32 devices in a mesh: pipe: 2 (over y), tx: 4 (over z), ty: 4 (over x, core).
Axes of the slice: x: 2, y: 2, z: 4, core: 2. Of those that a mesh axis runs over, the one named last changes fastest.
Arguments:
- section_input: bfloat16 [2, 48, 8192], P('pipe', 'tx', 'ty'), may hold values from -6 to 6
- saved_input: bfloat16 [2, 48, 8192], P('pipe', 'tx', 'ty'), may hold values from -6 to 6
- out_grad: bfloat16 [2, 48, 8192], P('pipe', 'tx', 'ty'), may hold values from -6 to 6
- gate_weight: bfloat16 [2, 8192, 29568], P('pipe', 'ty', 'tx'), may hold values from -0.0625 to 0.0625
- up_weight: bfloat16 [2, 8192, 29568], P('pipe', 'ty', 'tx'), may hold values from -0.0625 to 0.0625
- down_weight: bfloat16 [2, 29568, 8192], P('pipe', 'tx', 'ty'), may hold values from -0.03125 to 0.03125
Outputs:
- next_input: bfloat16 [2, 48, 8192], P('pipe', 'tx', 'ty')
- prev_grad: bfloat16 [2, 48, 8192], P('pipe', 'tx', 'ty')
The draws below stay inside these ranges and needn't reach their ends.
All inputs are finite; a program needn't handle non-finite values.
Results may differ from the reference program's by a relative error of at most 0.0038.
Values may be sent and summed in bfloat16 or wider, within the bound.
No kernel may reach another device: no remote copies, remote signals or barrier semaphores. Data moves between devices by JAX's collectives and lax.ppermute only.
A program may use at most 192 MiB of HBM per device.

```python
import jax
import jax.numpy as jnp
from jax import lax

D = 8192
FF = 29568
TOK = 48
SECTIONS = 2


def level_of(own_key, shape, pieces, smallest, top_value):
    loudness, own = 1.0, jax.random.fold_in(own_key, 6)
    for position, blocks in pieces:
        draws = jnp.exp(jax.random.uniform(jax.random.fold_in(own, position), (blocks,), jnp.float32, smallest / len(pieces), top_value / len(pieces)))
        loudness = loudness * jnp.repeat(draws, shape[position] // blocks).reshape([-1 if axis == position else 1 for axis in range(len(shape))])
    return loudness


def centred(rng, extent, width, bound, split=(), held_as=jnp.bfloat16):
    result = width * jax.random.normal(rng, extent, jnp.float32)
    if split:
        result = result * level_of(rng, extent, split, -0.22, 0.18)
    return jnp.clip(result, -bound, bound).astype(held_as)


def setup_inputs(seed: int = 0) -> dict:
    seeds = jax.random.split(jax.random.key(seed), 7)
    section_input = centred(seeds[0], (SECTIONS, TOK, D), 1.0, 6.0, ((0, 2), (1, 4), (2, 4)))
    saved_input = centred(seeds[1], (SECTIONS, TOK, D), 1.0, 6.0, ((0, 2), (1, 4), (2, 4)))
    out_grad = centred(seeds[2], (SECTIONS, TOK, D), 1.0, 6.0, ((0, 2), (1, 4), (2, 4)))
    gate_weight = centred(seeds[3], (SECTIONS, D, FF), D ** -0.5, 0.0625, ((0, 2), (1, 4), (2, 4)))
    up_weight = centred(seeds[4], (SECTIONS, D, FF), D ** -0.5, 0.0625, ((0, 2), (1, 4), (2, 4)))
    down_weight = centred(seeds[5], (SECTIONS, FF, D), FF ** -0.5, 0.03125, ((0, 2), (1, 4), (2, 4)))
    return dict(section_input=section_input, saved_input=saved_input, out_grad=out_grad, gate_weight=gate_weight, up_weight=up_weight, down_weight=down_weight)


def forward(inputs, wgate, wup, wdown):
    gate = jnp.dot(inputs, wgate, preferred_element_type=jnp.float32)
    up = jnp.dot(inputs, wup, preferred_element_type=jnp.float32)
    hidden = (jax.nn.silu(gate) * up).astype(jnp.bfloat16)
    mixed = jnp.dot(hidden, wdown, preferred_element_type=jnp.float32)
    return (inputs.astype(jnp.float32) + mixed).astype(jnp.bfloat16)


def backward(saved, grads, wgate, wup, wdown):
    dims = (((1,), (1,)), ((), ()))
    gate = jnp.dot(saved, wgate, preferred_element_type=jnp.float32)
    up = jnp.dot(saved, wup, preferred_element_type=jnp.float32)
    hidden_grad = lax.dot_general(grads, wdown, dims, preferred_element_type=jnp.float32)
    sigma = jax.nn.sigmoid(gate)
    gate_grad = (hidden_grad * up * sigma * (1.0 + gate * (1.0 - sigma))).astype(jnp.bfloat16)
    up_grad = (hidden_grad * gate * sigma).astype(jnp.bfloat16)
    total = grads.astype(jnp.float32)
    total = total + lax.dot_general(gate_grad, wgate, dims, preferred_element_type=jnp.float32)
    total = total + lax.dot_general(up_grad, wup, dims, preferred_element_type=jnp.float32)
    return total.astype(jnp.bfloat16)


def reference(section_input, saved_input, out_grad, gate_weight, up_weight, down_weight):
    outputs = []
    gradients = []
    for section in range(SECTIONS):
        outputs.append(forward(section_input[section], gate_weight[section], up_weight[section], down_weight[section]))
        gradients.append(backward(saved_input[section], out_grad[section], gate_weight[section], up_weight[section], down_weight[section]))
    next_input = jnp.roll(jnp.stack(outputs), 1, axis=0)
    prev_grad = jnp.roll(jnp.stack(gradients), -1, axis=0)
    return next_input, prev_grad
```

```python
import functools

import jax
import jax.numpy as jnp
from jax import lax
from jax.experimental import pallas as pl
from jax.experimental.pallas import tpu as pltpu
from jax.sharding import PartitionSpec as P

F32 = jnp.float32
BF16 = jnp.bfloat16
NN = (((1,), (0,)), ((), ()))
NT = (((1,), (1,)), ((), ()))
VM = pl.BlockSpec(memory_space=pltpu.VMEM)
HBM = pl.BlockSpec(memory_space=pltpu.HBM)
SM = pl.BlockSpec(memory_space=pltpu.SMEM)
STEP = 512
SLOTS = 5


def contract(a, b, dims):
    return lax.dot_general(a, b, dims, preferred_element_type=F32)


def params():
    return pltpu.CompilerParams(vmem_limit_bytes=4 * 2**20)


def cost(flops, moved):
    return pl.CostEstimate(flops=flops, bytes_accessed=moved, transcendentals=0)


def spans(size, step=STEP):
    return [(at, min(step, size - at)) for at in range(0, size, step)]


def up_to(value, unit):
    return -(-value // unit) * unit


def fetches(table_ref, stored, arena, loads, sems):
    copies = []
    for n, (at, rows, entry) in enumerate(loads):
        start = pl.multiple_of(table_ref[entry], 16)
        for i, source in enumerate(stored):
            target = arena.at[pl.ds(at + i * rows, rows), :]
            copies.append(pltpu.make_async_copy(source.at[pl.ds(start, rows), :], target, sems.at[n, i]))
    return copies


def begin(copies):
    for copy in copies:
        copy.start()


def end(copies):
    for copy in copies:
        copy.wait()


def call(body, operands, specs, shapes, arena, loads, table, stored, flops):
    body = functools.partial(body, loads)
    operands, specs, shapes = list(operands), list(specs), list(shapes)
    aliases, scratch, moved = {}, [], 0
    operands.append(table)
    specs.append(SM)
    if loads:
        operands += stored
        specs += [HBM] * 3
        scratch.append(pltpu.SemaphoreType.DMA((len(loads), 3)))
        moved = sum(6 * rows * stored[0].shape[1] for _, rows, _ in loads)
    if isinstance(arena, tuple):
        shape = arena
    else:
        shape = arena.shape
        aliases = {len(operands): len(shapes)}
        operands.append(arena)
        specs.append(VM)
    return pl.pallas_call(
        body,
        in_specs=specs,
        out_specs=[VM] * (len(shapes) + 1),
        out_shape=shapes + [pltpu.VMEM(shape, BF16)],
        scratch_shapes=scratch,
        input_output_aliases=aliases,
        compiler_params=params(),
        cost_estimate=cost(flops, moved),
    )(*operands)


def split(refs, loads, count, outs, carried):
    refs = list(refs)
    operands = refs[:count]
    table_ref, refs = refs[count], refs[count + 1 :]
    if loads:
        stored, refs = refs[:3], refs[3:]
    if carried:
        refs = refs[1:]
    results, arena = refs[:outs], refs[outs]
    copies = fetches(table_ref, stored, arena, loads, refs[outs + 1]) if loads else []
    return operands, results, arena, copies


def load_body(loads, *refs):
    copies = split(refs, loads, 0, 0, False)[3]
    begin(copies)
    end(copies)


def project_body(at, rows, has_more, loads, *refs):
    more, (out_ref,), arena, copies = split(refs, loads, has_more, 1, True)
    begin(copies)
    tokens = out_ref.shape[0] // 5
    base = arena.shape[0] - 3 * tokens
    for low, size in spans(rows):
        piece = pl.ds(low, size)
        for i, (first, count) in enumerate(((0, 2), (0, 2), (2, 1))):
            to = pl.ds(2 * i * tokens, count * tokens)
            lhs = arena[pl.ds(base + first * tokens, count * tokens), :]
            part = contract(lhs, arena[pl.ds(at + i * rows + low, size), :], NT)
            if has_more:
                part = part + more[0][to, piece]
            out_ref[to, piece] = part.astype(out_ref.dtype)
    end(copies)


def project(tokens, arena, slot, more, dtype, loads, table, stored):
    at, rows = slot
    width = arena.shape[1]
    operands = [more] if more is not None else []
    return call(
        functools.partial(project_body, at, rows, more is not None),
        operands,
        [VM] * len(operands),
        [jax.ShapeDtypeStruct((5 * tokens, rows), dtype)],
        arena,
        loads,
        table,
        stored,
        2 * 5 * tokens * rows * width,
    )


def activate_body(entry, others, loads, *refs):
    (own_ref, *got), (out_ref,), _, copies = split(refs, loads, 1 + others, 1, True)
    begin(copies)
    table_ref = refs[1 + others]
    t = own_ref.shape[0] // 5
    for low, size in spans(own_ref.shape[1], 256):
        piece = pl.ds(low, size)
        total = own_ref[:, piece]
        for ref in got:
            total = total + ref[:, piece].astype(F32)
        gate, saved_gate, up, saved_up, hidden_grad = [total[i * t : (i + 1) * t] for i in range(5)]
        column = lax.broadcasted_iota(jnp.int32, gate.shape, 1) + low
        mine = column >= table_ref[entry]
        hidden = gate * jax.nn.sigmoid(gate) * up
        sigma = jax.nn.sigmoid(saved_gate)
        gate_grad = hidden_grad * saved_up * sigma * (1.0 + saved_gate * (1.0 - sigma))
        up_grad = hidden_grad * saved_gate * sigma
        for i, value in enumerate((hidden, gate_grad, up_grad)):
            out_ref[i * t : (i + 1) * t, piece] = jnp.where(mine, value, 0.0).astype(BF16)
    end(copies)


def activate(entry, own, others, arena, loads, table, stored):
    rows, columns = own.shape
    operands = [own, *others]
    return call(
        functools.partial(activate_body, entry, len(others)),
        operands,
        [VM] * len(operands),
        [jax.ShapeDtypeStruct((rows // 5 * 3, columns), BF16)],
        arena,
        loads,
        table,
        stored,
        20 * rows * columns,
    )


def expand_body(slots, has_sum, parts, ends, loads, *refs):
    count = len(slots) + has_sum * len(parts)
    operands, outs, arena, copies = split(refs, loads, count, len(parts) * (1 + ends), True)
    begin(copies)
    held, sums = operands[: len(slots)], operands[len(slots) :]
    t = held[0].shape[0] // 3
    for low, size in spans(arena.shape[1]):
        piece = pl.ds(low, size)
        for i, part in enumerate(parts):
            value = sums[i][:, piece] if has_sum else 0.0
            for (at, rows), h_ref in zip(slots, held):
                for n in (0,) if part == "ahead" else (1, 2):
                    weight = arena[pl.ds(at + (n + 2) % 3 * rows, rows), piece]
                    value = value + contract(h_ref[pl.ds(n * t, t), :], weight, NN)
            if ends:
                outs[0][:, piece] = value[: t // 2]
                outs[1][:, piece] = value[t // 2 :].astype(BF16)
            else:
                outs[i][:, piece] = value
    end(copies)


def expand(held, arena, slots, sums, parts, ends, loads, table, stored):
    rows = sum(rows for _, rows in slots)
    t, width = held[0].shape[0] // 3, arena.shape[1]
    operands = held + (sums or [])
    shapes = [jax.ShapeDtypeStruct((t, width), F32)] * len(parts)
    if ends:
        shapes = [jax.ShapeDtypeStruct((t // 2, width), dtype) for dtype in (F32, BF16)]
    out = call(
        functools.partial(expand_body, slots, sums is not None, parts, ends),
        operands,
        [VM] * len(operands),
        shapes,
        arena,
        loads,
        table,
        stored,
        2 * (1 if len(parts) == 1 else 3) * t * rows * width,
    )
    return list(out[:-1]), out[-1]


def swap(value, axis, bit):
    return lax.ppermute(value, axis, [(i, i ^ bit) for i in range(lax.axis_size(axis))])


def to_chip(value, k):
    count = lax.axis_size("ty")
    return lax.ppermute(value, "ty", [(i, (i + 2 * k) % count) for i in range(count)])


def cross_pipe(value, step, bit):
    sections, count = lax.axis_size("pipe"), lax.axis_size("tx")
    pairs = [
        (p * count + i, (p + step) % sections * count + (i ^ bit))
        for p in range(sections)
        for i in range(count)
    ]
    return lax.ppermute(value, ("pipe", "tx"), pairs)


def finish(kept, gone, own, step):
    count = lax.axis_size("tx")
    t = own.shape[0]
    bit = 1
    while bit < count:
        if 2 * bit < count:
            kept = kept + swap(gone, "tx", bit).astype(F32)
            half = kept.shape[0] // 2
            kept, gone = kept[:half], kept[half:].astype(BF16)
        else:
            kept = cross_pipe(kept + own.astype(F32), step, 0) + cross_pipe(gone, step, bit).astype(F32)
        bit *= 2
    return kept.astype(BF16)


def gather_body(t, count, loads, *refs):
    blocks, _, arena, copies = split(refs, loads, count, 0, True)
    begin(copies)
    group = 16
    stack = jnp.concatenate([ref[...] for ref in blocks], axis=0)
    shape = (3 * count * t, stack.shape[0])
    row = lax.broadcasted_iota(jnp.int32, shape, 0)
    column = lax.broadcasted_iota(jnp.int32, shape, 1)
    kind, row = row // (count * t), row % (count * t)
    source = (row // t) * (3 * group) + kind * group + row % t
    pick = jnp.where(column == source, 1.0, 0.0).astype(BF16)
    base = arena.shape[0] - shape[0]
    for low, size in spans(stack.shape[1]):
        piece = pl.ds(low, size)
        arena[pl.ds(base, shape[0]), piece] = contract(pick, stack[:, low : low + size], NN).astype(BF16)
    end(copies)


def gathered(section, saved, grads, arena, loads, table, stored):
    count = lax.axis_size("tx")
    t, width = section.shape
    own = jnp.concatenate([jnp.pad(a, ((0, 16 - t), (0, 0))) for a in (section, saved, grads)])
    blocks = {0: own}
    bit = count // 2
    while bit:
        for i in list(blocks):
            blocks[i ^ bit] = swap(blocks[i], "tx", bit)
        bit //= 2
    bits = count.bit_length() - 1
    order = [int(format(n, f"0{bits}b")[::-1], 2) if bits else 0 for n in range(count)]
    operands = [blocks[i] for i in order]
    body = functools.partial(gather_body, t, count)
    return call(body, operands, [VM] * count, [], arena, loads, table, stored, 0)[0]


def residency(groups, slots, most):
    uses = [piece for group in groups for piece in group]

    def next_use(piece, after):
        return next((n for n in range(after, len(uses)) if uses[n] == piece), len(uses))

    begun = [(piece, slot) for slot, piece in enumerate(list(dict.fromkeys(uses))[:slots])]
    holds = {slot: piece for piece, slot in begun}
    loads_at, slot_at, after = [], [], 0
    for group in groups:
        after += len(group)
        slot_at.append([next(slot for slot, piece in holds.items() if piece == use) for use in group])
        loads = []
        for piece in dict.fromkeys(uses[after:]):
            if piece in holds.values() or len(loads) == most:
                continue
            slot = max((s for s in holds if s not in slot_at[-1]), key=lambda s: next_use(holds[s], after))
            if next_use(holds[slot], after) > next_use(piece, after):
                loads.append((piece, slot))
                holds[slot] = piece
        loads_at.append(loads)
    return begun, loads_at, slot_at


def local(section_input, saved_input, out_grad, gate_weight, up_weight, down_weight):
    count, tx = lax.axis_size("ty"), lax.axis_size("tx")
    chips = count // 2
    stored = [jnp.swapaxes(gate_weight[0], 0, 1), jnp.swapaxes(up_weight[0], 0, 1), down_weight[0]]
    units = up_to(stored[0].shape[0], 16)
    if units != stored[0].shape[0]:
        stored = [jnp.pad(w, ((0, units - w.shape[0]), (0, 0))) for w in stored]
    share = up_to(-(-units // count), 16)
    cut = share // 2 // 128 * 128
    subs = [(0, cut), (cut, share - cut)] if cut else [(0, share)]
    most = 3 * max(rows for _, rows in subs)

    me = lax.axis_index("ty")
    core, chip = me % 2, me // 2

    def share_of(k, mine):
        owner = (chip + k) % chips * 2 + (core if mine else 1 - core)
        return owner * share, jnp.minimum(owner * share, units - share)

    def place(k, mine, sub):
        return (share_of(k, mine)[1] + subs[sub][0]).astype(jnp.int32)

    def pieces(chip_order, core_order):
        return [(k, mine, sub) for k in chip_order for mine in core_order for sub in range(len(subs))]

    early = pieces(list(range(1, chips)) + [0], (False, True))
    late = pieces(range(chips), (True, False))
    groups = [[piece] for piece in early]
    groups += [late[n : n + len(subs)] for n in range(0, len(late), len(subs))]
    begun, loads_at, slot_at = residency(groups, SLOTS, 2)

    entries = {piece: n for n, piece in enumerate(early)}
    share_at, within = share_of(0, True)
    table = jnp.stack(
        [place(*piece) for piece in early]
        + [(share_at - within - at).astype(jnp.int32) for at, _ in subs]
    )

    def request(items):
        return [(slot * most, subs[piece[2]][1], entries[piece]) for piece, slot in items], table, stored

    tokens = tx * section_input.shape[1]
    (arena,) = call(load_body, [], [], [], (SLOTS * most + 3 * tokens, stored[0].shape[1]), *request(begun), 0)
    arena = gathered(section_input[0], saved_input[0], out_grad[0], arena, *request([]))
    passed, arrived, own = {}, {}, {}
    for n, (k, mine, sub) in enumerate(early):
        more = passed.pop((k, sub)) if mine else None
        dtype = BF16 if mine and k else F32
        slot = (slot_at[n][0] * most, subs[sub][1])
        part, arena = project(tokens, arena, slot, more, dtype, *request(loads_at[n]))
        if not mine:
            passed[k, sub] = swap(part, "ty", 1)
        elif k:
            arrived.setdefault(sub, []).append(to_chip(part, k))
        else:
            own[sub] = part

    h = {}
    for sub in range(len(subs)):
        h[0, True, sub], arena = activate(len(early) + sub, own[sub], arrived.get(sub, []), arena, *request([]))
        h[0, False, sub] = swap(h[0, True, sub], "ty", 1)
        for k in range(1, chips):
            h[k, True, sub] = to_chip(h[0, True, sub], chips - k)
            h[k, False, sub] = swap(h[k, True, sub], "ty", 1)

    sums = None
    both = ("ahead", "back")
    for n, group in enumerate(groups[len(early) :]):
        at = len(early) + n
        slots = [(slot * most, subs[piece[2]][1]) for slot, piece in zip(slot_at[at], group)]
        held = [h[piece] for piece in group]
        loads = request(loads_at[at])
        if at + 1 < len(groups):
            sums, arena = expand(held, arena, slots, sums, both, False, *loads)
        else:
            (kept, gone), arena = expand(held, arena, slots, sums[:1], both[:1], True, *loads)
            next_input = finish(kept, gone, section_input[0], 1)
            (kept, gone), arena = expand(held, arena, slots, sums[1:], both[1:], True, *request([]))
            prev_grad = finish(kept, gone, out_grad[0], -1)
    return (next_input[None], prev_grad[None])


def solution(mesh):
    return jax.shard_map(
        local,
        mesh=mesh,
        in_specs=(
            P("pipe", "tx", "ty"),
            P("pipe", "tx", "ty"),
            P("pipe", "tx", "ty"),
            P("pipe", "ty", "tx"),
            P("pipe", "ty", "tx"),
            P("pipe", "tx", "ty"),
        ),
        out_specs=(P("pipe", "tx", "ty"), P("pipe", "tx", "ty")),
        check_vma=False,
    )
```

```python
import functools

import jax
import jax.numpy as jnp
from jax import lax
from jax.experimental import pallas as pl
from jax.experimental.pallas import tpu as pltpu
from jax.sharding import PartitionSpec as P

F32 = jnp.float32
BF16 = jnp.bfloat16
NN = (((1,), (0,)), ((), ()))
NT = (((1,), (1,)), ((), ()))
VM = pl.BlockSpec(memory_space=pltpu.VMEM)
HBM = pl.BlockSpec(memory_space=pltpu.HBM)
SM = pl.BlockSpec(memory_space=pltpu.SMEM)
STEP = 512
SLOTS = 5
SPLIT = (2, 2, 1)
HINT = 2 * 10**9


def contract(a, b, dims):
    return lax.dot_general(a, b, dims, preferred_element_type=F32)


def params():
    return pltpu.CompilerParams(vmem_limit_bytes=62 * 2**20 // 10)


def spans(size, step=STEP):
    return [(at, min(step, size - at)) for at in range(0, size, step)]


def up_to(value, unit):
    return -(-value // unit) * unit


def fetches(table_ref, stored, arena, loads, sems):
    copies = []
    for n, (at, rows, entry, _) in enumerate(loads):
        start = pl.multiple_of(table_ref[entry], 16)
        for i, source in enumerate(stored):
            target = arena.at[pl.ds(at + i * rows, rows), :]
            copies.append(pltpu.make_async_copy(source.at[pl.ds(start, rows), :], target, sems.at[n, i]))
    return copies


def begin(copies):
    for copy in copies:
        copy.start()


def end(copies):
    for copy in copies:
        copy.wait()


def call(body, operands, shapes, scratch, arena, loads, table, stored, spec=HBM, weight=1):
    operands, specs = [*operands, table], [spec] * len(operands) + [SM]
    aliases, scratch = {}, list(scratch)
    if loads:
        operands += stored
        specs += [HBM] * 3
        scratch.append(pltpu.SemaphoreType.DMA((len(loads), 3)))
    held = []
    if isinstance(arena, tuple):
        held = [pltpu.VMEM(arena, BF16)]
    elif arena is not None:
        held = [pltpu.VMEM(arena.shape, BF16)]
        aliases = {len(operands): len(shapes)}
        operands.append(arena)
        specs.append(VM)
    return pl.pallas_call(
        functools.partial(body, loads),
        in_specs=specs,
        out_specs=[spec] * len(shapes) + [VM] * len(held),
        out_shape=list(shapes) + held,
        scratch_shapes=scratch,
        input_output_aliases=aliases,
        compiler_params=params(),
        cost_estimate=pl.CostEstimate(flops=weight * HINT, bytes_accessed=0, transcendentals=0),
    )(*operands)


def split(refs, loads, count, outs, carried=True):
    operands, table, refs = refs[:count], refs[count], refs[count + 1 :]
    if loads:
        stored, refs = refs[:3], refs[3:]
    if carried:
        refs = refs[1:]
    results, arena, scratch = refs[:outs], refs[outs], refs[outs + 1 :]
    if carried is None:
        arena, scratch = None, refs[outs:]
    copies = []
    if loads:
        copies, scratch = fetches(table, stored, arena, loads, scratch[-1]), scratch[:-1]
    return operands, table, results, arena, scratch, copies


def load_body(carried, loads, *refs):
    copies = split(refs, loads, 0, 0, carried)[-1]
    begin(copies)
    end(copies)


def load(arena, loads, table, stored):
    carried = not isinstance(arena, tuple)
    return call(functools.partial(load_body, carried), [], [], [], arena, loads, table, stored)[0]


def products(arena, h_refs, slots, part, tokens, piece):
    value = 0.0
    for h_ref, (at, rows) in zip(h_refs, slots):
        for i in (1, 2) if part else (0,):
            lhs = h_ref[pl.ds(i * tokens, tokens), :]
            value = value + contract(lhs, arena[pl.ds(at + (i + 2) % 3 * rows, rows), piece], NN)
    return value


def sum_rows(arena, part, tokens):
    low = arena.shape[0] - 4 * tokens + 2 * part * tokens
    return pl.ds(low, tokens), pl.ds(low + tokens, tokens)


def keep(arena, value, part, tokens, piece):
    high, low = sum_rows(arena, part, tokens)
    rounded = value.astype(BF16)
    arena[high, piece] = rounded
    arena[low, piece] = (value - rounded.astype(F32)).astype(BF16)


def kept_sum(arena, part, tokens, piece):
    high, low = sum_rows(arena, part, tokens)
    return arena[high, piece].astype(F32) + arena[low, piece].astype(F32)


def project_body(at, rows, got, others, leave, tokens, entry, fresh, loads, *refs):
    outs = 1 if entry is not None else len(leave)
    operands, table, out_refs, arena, scratch, copies = split(refs, loads, len(got) + others, outs)
    part_ref, out_sems = scratch[:2]
    blocks = [pl.ds(0, 2 * tokens), pl.ds(2 * tokens, 2 * tokens), pl.ds(4 * tokens, tokens)]
    arrivals, held = [], scratch[2 : 2 + others + (1 if got else 0)]
    in_sems = scratch[2 + len(held)] if held else None
    targets, low = [], 0
    for count in got:
        targets.append(held[0].at[pl.ds(low, count * tokens), :])
        low += count * tokens
    targets += held[1 if got else 0 :]
    arrivals = [pltpu.make_async_copy(source, targets[i], in_sems.at[i]) for i, source in enumerate(operands)]
    begin(arrivals)
    if not arrivals:
        begin(copies)
    first_ref = scratch[-1] if arrivals and entry is None else part_ref
    h_ref = scratch[-1]
    base = arena.shape[0] - 7 * tokens
    leaving = []

    def finished(part, i, piece):
        for ref in held:
            part = part + ref[blocks[i], piece].astype(F32)
        return part

    def leaves(i):
        if entry is None:
            target = out_refs[0].at[blocks[i], :] if len(out_refs) == 1 else out_refs[i]
            leaving.append(pltpu.make_async_copy(part_ref.at[blocks[i], :], target, out_sems.at[i]))
            leaving[-1].start()

    for i, (first, count) in enumerate(((0, 2), (0, 2), (2, 1))):
        lhs = arena[pl.ds(base + first * tokens, count * tokens), :]
        for low, size in spans(rows):
            piece = pl.ds(low, size)
            part = contract(lhs, arena[pl.ds(at + i * rows + low, size), :], NT)
            if not i and arrivals:
                first_ref[blocks[0], piece] = part
                continue
            if i == 1 and not low and arrivals:
                end(arrivals)
                begin(copies)
            part_ref[blocks[i], piece] = finished(part, i, piece).astype(part_ref.dtype)
            if i == 2 and entry is not None:
                for at_column in range(low, low + size, 128):
                    columns = pl.ds(at_column, min(128, low + size - at_column))
                    gate, saved_gate, up, saved_up, hidden_grad = [
                        part_ref[pl.ds(n * tokens, tokens), columns] for n in range(5)
                    ]
                    mine = lax.broadcasted_iota(jnp.int32, gate.shape, 1) + at_column >= table[entry]
                    hidden = gate * jax.nn.sigmoid(gate) * up
                    sigma = jax.nn.sigmoid(saved_gate)
                    gate_grad = hidden_grad * saved_up * sigma * (1.0 + saved_gate * (1.0 - sigma))
                    up_grad = hidden_grad * saved_gate * sigma
                    for n, value in enumerate((hidden, gate_grad, up_grad)):
                        h_ref[pl.ds(n * tokens, tokens), columns] = jnp.where(mine, value, 0.0).astype(BF16)
        if i == 1 and arrivals:
            for low, size in spans(rows):
                piece = pl.ds(low, size)
                part = finished(first_ref[blocks[0], piece], 0, piece)
                part_ref[blocks[0], piece] = part.astype(part_ref.dtype)
            leaves(0)
        if i or not arrivals:
            leaves(i)
    if entry is not None:
        leaving.append(pltpu.make_async_copy(h_ref, out_refs[0], out_sems.at[0]))
        leaving[-1].start()
        for low, size in spans(arena.shape[1]):
            piece = pl.ds(low, size)
            for part in (0, 1):
                value = products(arena, [h_ref], [(at, rows)], part, tokens, piece)
                if not fresh:
                    value = value + kept_sum(arena, part, tokens, piece)
                keep(arena, value, part, tokens, piece)
    end(leaving)
    end(copies)


def project(tokens, arena, slot, more, others, leave, dtype, entry, fresh, loads, table, stored):
    at, rows = slot
    operands = more + others
    part = jax.ShapeDtypeStruct((5 * tokens, rows), dtype)
    shapes = [jax.ShapeDtypeStruct((count * tokens, rows), dtype) for count in leave]
    if entry is not None:
        shapes = [jax.ShapeDtypeStruct((3 * tokens, rows), BF16)]
    scratch = [pltpu.VMEM(part.shape, dtype), pltpu.SemaphoreType.DMA((3,))]
    scratch += [pltpu.VMEM(part.shape, F32)] * (1 if more else 0)
    scratch += [pltpu.VMEM(operand.shape, operand.dtype) for operand in others]
    if operands:
        scratch.append(pltpu.SemaphoreType.DMA((len(operands),)))
    if entry is not None:
        scratch.append(pltpu.VMEM(shapes[0].shape, BF16))
    elif operands:
        scratch.append(pltpu.VMEM((2 * tokens, rows), F32))
    got = [piece.shape[0] // tokens for piece in more]
    body = functools.partial(project_body, at, rows, got, len(others), leave, tokens, entry, fresh)
    *outs, arena = call(body, operands, shapes, scratch, arena, loads, table, stored, HBM, 1 if entry is None else 2)
    return outs, arena


def expand_body(slots, parts, ends, tokens, loads, *refs):
    operands, _, outs, arena, scratch, copies = split(refs, loads, len(slots), 2 * ends)
    in_sems, out_sems, *held = scratch
    arrivals = [pltpu.make_async_copy(operand, held[i], in_sems.at[i]) for i, operand in enumerate(operands)]
    begin(arrivals)
    total_ref, gone_ref = held[len(slots) :] if ends else (None, None)
    leaving = []
    for n, slot in enumerate(slots):
        if not n:
            end(arrivals)
        for i, copy in enumerate(copies):
            if loads[i // 3][3] == n:
                copy.start()
        for m, (low, size) in enumerate(spans(arena.shape[1])):
            piece = pl.ds(low, size)
            for part in parts:
                value = products(arena, [held[n]], [slot], part, tokens, piece)
                value = value + kept_sum(arena, part, tokens, piece)
                if not ends or n < len(slots) - 1:
                    keep(arena, value, part, tokens, piece)
                    continue
                total_ref[:, piece] = value[: tokens // 2]
                gone_ref[:, piece] = value[tokens // 2 :].astype(BF16)
                for k, source in enumerate((total_ref, gone_ref)):
                    copy = pltpu.make_async_copy(source.at[:, piece], outs[k].at[:, piece], out_sems.at[k, m])
                    leaving.append(copy)
                    copy.start()
    end(leaving)
    end(copies)


def expand(tokens, held, arena, slots, parts, ends, loads, table, stored):
    width = arena.shape[1]
    shapes = []
    scratch = [pltpu.SemaphoreType.DMA((len(held),)), pltpu.SemaphoreType.DMA((2, len(spans(width))))]
    scratch += [pltpu.VMEM(operand.shape, operand.dtype) for operand in held]
    if ends:
        shapes = [jax.ShapeDtypeStruct((tokens // 2, width), dtype) for dtype in (F32, BF16)]
        scratch += [pltpu.VMEM(shape.shape, shape.dtype) for shape in shapes]
    body = functools.partial(expand_body, slots, parts, ends, tokens)
    *outs, arena = call(body, held, shapes, scratch, arena, loads, table, stored)
    return outs, arena


def swap(value, axis, bit):
    return lax.ppermute(value, axis, [(i, i ^ bit) for i in range(lax.axis_size(axis))])


def to_chip(value, k):
    count = lax.axis_size("ty")
    return lax.ppermute(value, "ty", [(i, (i + 2 * k) % count) for i in range(count)])


def cross_pipe(value, step, bit):
    sections, count = lax.axis_size("pipe"), lax.axis_size("tx")
    pairs = [
        (p * count + i, (p + step) % sections * count + (i ^ bit))
        for p in range(sections)
        for i in range(count)
    ]
    return lax.ppermute(value, ("pipe", "tx"), pairs)


def meet_body(last, carried, loads, *refs):
    operands, _, (near_ref, gone_ref), _, (total_ref,), _ = split(refs, loads, 3, 2, carried)
    kept_ref, got_ref, own_ref = operands
    half = near_ref.shape[0]
    total_ref[...] = kept_ref[...] + got_ref[...].astype(F32)
    near = total_ref[pl.ds(0, half), :]
    near_ref[...] = near + own_ref[...].astype(F32) if last else near
    gone_ref[...] = total_ref[pl.ds(half, half), :].astype(BF16)


def meet(kept, got, own, last, arena, table, stored):
    half, width = kept.shape[0] // 2, kept.shape[1]
    shapes = [jax.ShapeDtypeStruct((half, width), dtype) for dtype in (F32, BF16)]
    scratch = [pltpu.VMEM(kept.shape, F32)]
    body = functools.partial(meet_body, last, None if arena is None else True)
    near, gone, *arena = call(body, [kept, got, own], shapes, scratch, arena, [], table, stored, VM)
    return near, gone, arena[0] if arena else None


def finish(kept, got, own, step, arena, table, stored):
    count = lax.axis_size("tx")
    bit = 1
    while 2 * bit < count:
        bit *= 2
        kept, gone, arena = meet(kept, got, own, 2 * bit == count, arena, table, stored)
        if 2 * bit < count:
            got = swap(gone, "tx", bit)
    far = cross_pipe(gone, step, bit).astype(F32)
    return (cross_pipe(kept, step, 0) + far).astype(BF16), arena


def gather_body(t, count, loads, *refs):
    operands, _, _, arena, _, copies = split(refs, loads, count, 0)
    begin(copies)
    shape = (3 * count * t, 3 * t)
    row = lax.broadcasted_iota(jnp.int32, shape, 0)
    column = lax.broadcasted_iota(jnp.int32, shape, 1)
    kind, row = row // (count * t), row % (count * t)
    source = kind * t + row % t
    picks = [
        jnp.where((row // t == i) & (column == source), 1.0, 0.0).astype(BF16) for i in range(count)
    ]
    base = arena.shape[0] - 7 * count * t
    for low, size in spans(arena.shape[1]):
        piece = pl.ds(low, size)
        rows = sum(contract(pick, operand[:, piece], NN) for pick, operand in zip(picks, operands))
        arena[pl.ds(base, shape[0]), piece] = rows.astype(BF16)
    end(copies)


def after(value, others):
    return lax.optimization_barrier((value, others))[0]


def gathered(section, saved, grads, shape, loads, table, stored):
    count = lax.axis_size("tx")
    t = section.shape[0]
    own = jnp.concatenate([section, saved, grads])
    bit = count // 2
    blocks, near = {0: own}, None
    if count > 1:
        near = swap(own, "tx", 1)
    arena = load(shape, loads[:-1], table, stored)
    while bit > 1:
        for i in list(blocks):
            blocks[i ^ bit] = swap(blocks[i], "tx", bit)
        bit //= 2
    if count > 1:
        far = [i for i in blocks if i]
        for i in far:
            blocks[i ^ 1] = swap(after(blocks[i], arena), "tx", 1)
        blocks[1] = near
    arena = load(arena, loads[-1:], table, stored)
    bits = count.bit_length() - 1
    order = [int(format(n, f"0{bits}b")[::-1], 2) if bits else 0 for n in range(count)]
    operands = [blocks[i] for i in order]
    body = functools.partial(gather_body, t, count)
    return call(body, operands, [], [], arena, [], table, stored, VM)[0]


def residency(groups, quiet, slots, first):
    uses = [piece for group in groups for piece in group]

    def next_use(piece, at):
        return next((n for n in range(at, len(uses)) if uses[n] == piece), len(uses))

    begun = [(piece, slot, 0) for slot, piece in enumerate(list(dict.fromkeys(uses))[:first])]
    holds = {slot: None for slot in range(slots)}
    holds.update((slot, piece) for piece, slot, _ in begun)
    loads_at, slot_at, at = [], [], 0
    for step, group in enumerate(groups):
        slot_at.append([next(slot for slot, piece in holds.items() if piece == use) for use in group])
        loads = []
        later = at + len(group)
        for stage in range(len(group)):
            busy = slot_at[-1][stage:]
            while True:
                wanted = next((p for p in uses[later:] if p not in holds.values()), None)
                urgent = step + 1 < len(groups) and wanted in groups[step + 1]
                free = [s for s in holds if s not in busy and s not in [slot for _, slot, _ in loads]]
                if wanted is None or not free or (loads or step in quiet) and not urgent:
                    break
                slot = max(free, key=lambda s: next_use(holds[s], later))
                if next_use(holds[slot], later) <= next_use(wanted, later):
                    break
                loads.append((wanted, slot, stage))
                holds[slot] = wanted
        loads_at.append(loads)
        at += len(group)
    return begun, loads_at, slot_at


def local(section_input, saved_input, out_grad, gate_weight, up_weight, down_weight):
    count, tx = lax.axis_size("ty"), lax.axis_size("tx")
    chips = count // 2
    stored = [jnp.swapaxes(gate_weight[0], 0, 1), jnp.swapaxes(up_weight[0], 0, 1), down_weight[0]]
    units = up_to(stored[0].shape[0], 16)
    if units != stored[0].shape[0]:
        stored = [jnp.pad(w, ((0, units - w.shape[0]), (0, 0))) for w in stored]
    share = up_to(-(-units // count), 16)
    cut = share - share // 2 // 128 * 128
    subs = [(0, cut), (cut, share - cut)] if cut < share else [(0, share)]
    most = 3 * max(rows for _, rows in subs)

    me = lax.axis_index("ty")
    core, chip = me % 2, me // 2

    def share_of(k, mine):
        owner = (chip + k) % chips * 2 + (core if mine else 1 - core)
        return owner * share, jnp.minimum(owner * share, units - share)

    def place(k, mine, sub):
        return (share_of(k, mine)[1] + subs[sub][0]).astype(jnp.int32)

    def pieces(chip_order, core_order):
        return [(k, mine, sub) for k in chip_order for mine in core_order for sub in range(len(subs))]

    steps = [("project", [piece]) for piece in pieces(range(1, chips), (False, True)) + pieces((0,), (False,))]
    steps += [("activate", [piece]) for piece in pieces((0,), (True,))]
    left = pieces((0,), (False,)) + pieces(range(1, chips), (True, False))
    last = min(len(left) - 1, len(subs) + 1)
    steps.append(("expand", left[:1]))
    steps += [("expand", left[n : min(n + 2, len(left) - last)]) for n in range(1, len(left) - last, 2)]
    steps.append(("end", left[-last:]))
    quiet = [n for n, (kind, group) in enumerate(steps) if kind == "project" and group[0][1]]
    begun, loads_at, slot_at = residency([group for _, group in steps], quiet, SLOTS, SLOTS - 2)

    entries = {piece: n for n, piece in enumerate(pieces(range(chips), (False, True)))}
    share_at, within = share_of(0, True)
    table = jnp.stack(
        [place(*piece) for piece in entries]
        + [(share_at - within - at).astype(jnp.int32) for at, _ in subs]
    )

    def request(items):
        loads = [(slot * most, subs[piece[2]][1], entries[piece], stage) for piece, slot, stage in items]
        return loads, table, stored

    tokens = tx * section_input.shape[1]
    shape = (SLOTS * most + 7 * tokens, stored[0].shape[1])
    arena = gathered(section_input[0], saved_input[0], out_grad[0], shape, *request(begun))
    passed, arrived, h, forwarded = {}, {}, {}, chips == 1
    for n, (kind, group) in enumerate(steps):
        slots = [(slot * most, subs[piece[2]][1]) for slot, piece in zip(slot_at[n], group)]
        loads = request(loads_at[n])
        k, mine, sub = group[0]
        if kind == "project":
            more = passed.pop((k, sub)) if mine else []
            leave, dtype = ((5,), BF16) if mine else ((5,) if k else SPLIT, F32)
            parts, arena = project(tokens, arena, slots[0], more, [], leave, dtype, None, False, *loads)
            if mine:
                arrived.setdefault(sub, []).append(to_chip(parts[0], k))
            else:
                passed[k, sub] = [swap(part, "ty", 1) for part in parts]
        elif kind == "activate":
            others, entry = arrived.get(sub, []), len(entries) + sub
            more = passed.pop((k, sub))
            (own,), arena = project(tokens, arena, slots[0], more, others, (), F32, entry, not sub, *loads)
            h[0, True, sub] = own
            for i in range(1, chips):
                h[i, True, sub] = to_chip(own, chips - i)
            h[0, False, sub] = swap(own, "ty", 1)
        elif kind == "expand":
            held = [h[piece] for piece in group]
            _, arena = expand(tokens, held, arena, slots, (0, 1), False, *loads)
            if not forwarded and len(h) == len(subs) * (chips + 1):
                forwarded = True
                for i in range(1, chips):
                    for j in range(len(subs)):
                        h[i, False, j] = swap(after(h[i, True, j], arena), "ty", 1)
        else:
            if not forwarded:
                for i in range(1, chips):
                    for j in range(len(subs)):
                        h[i, False, j] = swap(h[i, True, j], "ty", 1)
            held = [h[piece] for piece in group]
            (kept, gone), arena = expand(tokens, held, arena, slots, (0,), True, *loads)
            got = swap(gone, "tx", 1)
            _, arena = expand(tokens, held[:-1], arena, slots[:-1], (1,), False, *request([]))
            next_input, arena = finish(kept, got, section_input[0], 1, arena, table, stored)
            (kept, gone), arena = expand(tokens, held[-1:], arena, slots[-1:], (1,), True, *request([]))
            got = swap(gone, "tx", 1)
            prev_grad, _ = finish(after(kept, next_input), got, out_grad[0], -1, None, table, stored)
    return (next_input[None], prev_grad[None])


def solution(mesh):
    return jax.shard_map(
        local,
        mesh=mesh,
        in_specs=(
            P("pipe", "tx", "ty"),
            P("pipe", "tx", "ty"),
            P("pipe", "tx", "ty"),
            P("pipe", "ty", "tx"),
            P("pipe", "ty", "tx"),
            P("pipe", "tx", "ty"),
        ),
        out_specs=(P("pipe", "tx", "ty"), P("pipe", "tx", "ty")),
        check_vma=False,
    )
```

```python
import functools

import jax
import jax.numpy as jnp
from jax import lax
from jax.experimental import pallas as pl
from jax.experimental.pallas import tpu as pltpu
from jax.sharding import PartitionSpec as P

F32 = jnp.float32
BF16 = jnp.bfloat16
NN = (((1,), (0,)), ((), ()))
NT = (((1,), (1,)), ((), ()))
VM = pl.BlockSpec(memory_space=pltpu.VMEM)
HBM = pl.BlockSpec(memory_space=pltpu.HBM)
SM = pl.BlockSpec(memory_space=pltpu.SMEM)
STEP = 512
SLOTS = 5
BEGUN = 2
SPLIT = (2, 2, 1)
HINT = 2 * 10**9


def contract(a, b, dims):
    return lax.dot_general(a, b, dims, preferred_element_type=F32)


def params():
    return pltpu.CompilerParams(vmem_limit_bytes=62 * 2**20 // 10)


def spans(size, step=STEP):
    return [(at, min(step, size - at)) for at in range(0, size, step)]


def up_to(value, unit):
    return -(-value // unit) * unit


def fetches(table_ref, stored, arena, loads, sems):
    copies = []
    for n, (at, rows, entry, _) in enumerate(loads):
        start = pl.multiple_of(table_ref[entry], 16)
        for i, source in enumerate(stored):
            target = arena.at[pl.ds(at + i * rows, rows), :]
            copies.append(pltpu.make_async_copy(source.at[pl.ds(start, rows), :], target, sems.at[n, i]))
    return copies


def begin(copies):
    for copy in copies:
        copy.start()


def end(copies):
    for copy in copies:
        copy.wait()


def call(body, operands, shapes, scratch, arena, loads, table, stored, spec=HBM, weight=1):
    operands, specs = [*operands, table], [spec] * len(operands) + [SM]
    aliases, scratch = {}, list(scratch)
    if loads:
        operands += stored
        specs += [HBM] * 3
        scratch.append(pltpu.SemaphoreType.DMA((len(loads), 3)))
    held = []
    if isinstance(arena, tuple):
        held = [pltpu.VMEM(arena, BF16)]
    elif arena is not None:
        held = [pltpu.VMEM(arena.shape, BF16)]
        aliases = {len(operands): len(shapes)}
        operands.append(arena)
        specs.append(VM)
    return pl.pallas_call(
        functools.partial(body, loads),
        in_specs=specs,
        out_specs=[spec] * len(shapes) + [VM] * len(held),
        out_shape=list(shapes) + held,
        scratch_shapes=scratch,
        input_output_aliases=aliases,
        compiler_params=params(),
        cost_estimate=pl.CostEstimate(flops=weight * HINT, bytes_accessed=0, transcendentals=0),
    )(*operands)


def split(refs, loads, count, outs, carried=True):
    operands, table, refs = refs[:count], refs[count], refs[count + 1 :]
    if loads:
        stored, refs = refs[:3], refs[3:]
    if carried:
        refs = refs[1:]
    results, arena, scratch = refs[:outs], refs[outs], refs[outs + 1 :]
    if carried is None:
        arena, scratch = None, refs[outs:]
    copies = []
    if loads:
        copies, scratch = fetches(table, stored, arena, loads, scratch[-1]), scratch[:-1]
    return operands, table, results, arena, scratch, copies


def load_body(carried, loads, *refs):
    copies = split(refs, loads, 0, 0, carried)[-1]
    begin(copies)
    end(copies)


def load(arena, loads, table, stored):
    carried = not isinstance(arena, tuple)
    return call(functools.partial(load_body, carried), [], [], [], arena, loads, table, stored)[0]


def products(arena, h_refs, slots, part, tokens, piece):
    value = 0.0
    for h_ref, (at, rows) in zip(h_refs, slots):
        for i in (1, 2) if part else (0,):
            lhs = h_ref[pl.ds(i * tokens, tokens), :]
            value = value + contract(lhs, arena[pl.ds(at + (i + 2) % 3 * rows, rows), piece], NN)
    return value


def sum_rows(arena, part, tokens):
    low = arena.shape[0] - 4 * tokens + 2 * part * tokens
    return pl.ds(low, tokens), pl.ds(low + tokens, tokens)


def keep(arena, value, part, tokens, piece):
    high, low = sum_rows(arena, part, tokens)
    rounded = value.astype(BF16)
    arena[high, piece] = rounded
    arena[low, piece] = (value - rounded.astype(F32)).astype(BF16)


def kept_sum(arena, part, tokens, piece):
    high, low = sum_rows(arena, part, tokens)
    return arena[high, piece].astype(F32) + arena[low, piece].astype(F32)


def project_body(jobs, tokens, loads, *refs):
    ins = sum(len(job["got"]) + job["others"] for job in jobs)
    outs = sum(len(job["leave"]) or 1 for job in jobs)
    operands, table, out_refs, arena, scratch, copies = split(refs, loads, ins, outs)
    operands, out_refs, scratch = list(operands), list(out_refs), list(scratch)
    blocks = [pl.ds(0, 2 * tokens), pl.ds(2 * tokens, 2 * tokens), pl.ds(4 * tokens, tokens)]
    base = arena.shape[0] - 7 * tokens
    work = []
    for job in jobs:
        part_ref, out_sems = scratch.pop(0), scratch.pop(0)
        held = [scratch.pop(0) for _ in range(job["others"] + bool(job["got"]))]
        targets, low = [], 0
        for count in job["got"]:
            targets.append(held[0].at[pl.ds(low, count * tokens), :])
            low += count * tokens
        targets += held[bool(job["got"]) :]
        in_sems = scratch.pop(0) if targets else None
        arrivals = [
            pltpu.make_async_copy(operands.pop(0), target, in_sems.at[i]) for i, target in enumerate(targets)
        ]
        begin(arrivals)
        h_ref = scratch.pop(0) if job["entry"] is not None else None
        first_ref = part_ref
        if targets and h_ref is None:
            first_ref = scratch.pop(0)
        to = [out_refs.pop(0) for _ in range(len(job["leave"]) or 1)]
        work.append((job, part_ref, out_sems, held, arrivals, h_ref, first_ref, to))
    if not work[0][4]:
        begin(copies)
    leaving = []

    for number, (job, part_ref, out_sems, held, arrivals, h_ref, first_ref, to) in enumerate(work):
        at, rows, entry = job["at"], job["rows"], job["entry"]
        pending = (0, 1, 2) if copies and entry is None and len(work) == 1 else (0,)
        pending = pending if arrivals else ()
        if arrivals and pending == (0, 1, 2) and not number:
            begin(copies)

        def finished(part, i, piece):
            for ref in held:
                part = part + ref[blocks[i], piece].astype(F32)
            return part

        def complete(i):
            for low, size in spans(rows):
                piece = pl.ds(low, size)
                part = finished(first_ref[blocks[i], piece], i, piece)
                part_ref[blocks[i], piece] = part.astype(part_ref.dtype)

        def leaves(i):
            if entry is None:
                target = to[0].at[blocks[i], :] if len(to) == 1 else to[i]
                leaving.append(pltpu.make_async_copy(part_ref.at[blocks[i], :], target, out_sems.at[i]))
                leaving[-1].start()

        for i, (first, count) in enumerate(((0, 2), (0, 2), (2, 1))):
            lhs = arena[pl.ds(base + first * tokens, count * tokens), :]
            for low, size in spans(rows):
                piece = pl.ds(low, size)
                part = contract(lhs, arena[pl.ds(at + i * rows + low, size), :], NT)
                if i in pending:
                    first_ref[blocks[i], piece] = part
                    continue
                if pending and i == 1 and not low:
                    end(arrivals)
                    if not number:
                        begin(copies)
                part_ref[blocks[i], piece] = finished(part, i, piece).astype(part_ref.dtype)
                if i < 2 or entry is None:
                    continue
                for at_column in range(low, low + size, 128):
                    columns = pl.ds(at_column, min(128, low + size - at_column))
                    gate, saved_gate, up, saved_up, hidden_grad = [
                        part_ref[pl.ds(n * tokens, tokens), columns] for n in range(5)
                    ]
                    mine = lax.broadcasted_iota(jnp.int32, gate.shape, 1) + at_column >= table[entry]
                    hidden = gate * jax.nn.sigmoid(gate) * up
                    sigma = jax.nn.sigmoid(saved_gate)
                    gate_grad = hidden_grad * saved_up * sigma * (1.0 + saved_gate * (1.0 - sigma))
                    up_grad = hidden_grad * saved_gate * sigma
                    for n, value in enumerate((hidden, gate_grad, up_grad)):
                        h_ref[pl.ds(n * tokens, tokens), columns] = jnp.where(mine, value, 0.0).astype(BF16)
            if i == 1 and pending == (0,):
                complete(0)
                leaves(0)
            if i not in pending:
                leaves(i)
        if pending == (0, 1, 2):
            end(arrivals)
            for i in pending:
                complete(i)
                leaves(i)
        if entry is not None:
            leaving.append(pltpu.make_async_copy(h_ref, to[0], out_sems.at[0]))
            leaving[-1].start()
            for low, size in spans(arena.shape[1]):
                piece = pl.ds(low, size)
                for part in (0, 1):
                    value = products(arena, [h_ref], [(at, rows)], part, tokens, piece)
                    if not job["fresh"]:
                        value = value + kept_sum(arena, part, tokens, piece)
                    keep(arena, value, part, tokens, piece)
    end(leaving)
    end(copies)


def project(tokens, arena, jobs, loads, table, stored):
    operands, shapes, scratch, static = [], [], [], []
    for (at, rows), more, others, leave, dtype, entry, fresh in jobs:
        operands += more + others
        part = jax.ShapeDtypeStruct((5 * tokens, rows), dtype)
        scratch += [pltpu.VMEM(part.shape, dtype), pltpu.SemaphoreType.DMA((3,))]
        scratch += [pltpu.VMEM(part.shape, F32)] * (1 if more else 0)
        scratch += [pltpu.VMEM(operand.shape, operand.dtype) for operand in others]
        if more or others:
            scratch.append(pltpu.SemaphoreType.DMA((len(more + others),)))
        if entry is not None:
            shapes.append(jax.ShapeDtypeStruct((3 * tokens, rows), BF16))
            scratch.append(pltpu.VMEM(shapes[-1].shape, BF16))
        else:
            shapes += [jax.ShapeDtypeStruct((count * tokens, rows), dtype) for count in leave]
            if more or others:
                scratch.append(pltpu.VMEM(part.shape, F32))
        got = [piece.shape[0] // tokens for piece in more]
        static.append(dict(at=at, rows=rows, got=got, others=len(others), leave=leave, entry=entry, fresh=fresh))
    weight = sum(1 if job["entry"] is None else 2 for job in static)
    body = functools.partial(project_body, static, tokens)
    *outs, arena = call(body, operands, shapes, scratch, arena, loads, table, stored, weight=weight)
    return outs, arena


def expand_body(slots, parts, ends, tokens, loads, *refs):
    operands, _, outs, arena, scratch, copies = split(refs, loads, len(slots), 2 * ends)
    in_sems, *held = scratch
    arrivals = [pltpu.make_async_copy(operand, held[i], in_sems.at[i]) for i, operand in enumerate(operands)]
    begin(arrivals)
    leaving = []
    if ends:
        out_sems, *leave_refs = held[len(slots) :]
    for n, slot in enumerate(slots):
        if not n and len(slots) > 1:
            end(arrivals)
        for i, copy in enumerate(copies):
            if loads[i // 3][3] == n:
                copy.start()
        if not n and len(slots) == 1:
            end(arrivals)
        for m, (low, size) in enumerate(spans(arena.shape[1])):
            piece = pl.ds(low, size)
            for part in parts:
                value = products(arena, [held[n]], [slot], part, tokens, piece)
                value = value + kept_sum(arena, part, tokens, piece)
                if not ends or n < len(slots) - 1:
                    keep(arena, value, part, tokens, piece)
                    continue
                leave_refs[0][:, piece] = value[: tokens // 2]
                leave_refs[1][:, piece] = value[tokens // 2 :].astype(BF16)
                for k, source in enumerate(leave_refs):
                    copy = pltpu.make_async_copy(source.at[:, piece], outs[k].at[:, piece], out_sems.at[k, m])
                    leaving.append(copy)
                    copy.start()
    end(leaving)
    end(copies)


def expand(tokens, held, arena, slots, parts, ends, loads, table, stored):
    width = arena.shape[1]
    shapes = []
    scratch = [pltpu.SemaphoreType.DMA((len(held),))]
    scratch += [pltpu.VMEM(operand.shape, operand.dtype) for operand in held]
    if ends:
        shapes = [jax.ShapeDtypeStruct((tokens // 2, width), dtype) for dtype in (F32, BF16)]
        scratch.append(pltpu.SemaphoreType.DMA((2, len(spans(width)))))
        scratch += [pltpu.VMEM(shape.shape, shape.dtype) for shape in shapes]
    body = functools.partial(expand_body, slots, parts, ends, tokens)
    *outs, arena = call(body, held, shapes, scratch, arena, loads, table, stored)
    return outs, arena


def swap(value, axis, bit):
    return lax.ppermute(value, axis, [(i, i ^ bit) for i in range(lax.axis_size(axis))])


def to_chip(value, k):
    count = lax.axis_size("ty")
    return lax.ppermute(value, "ty", [(i, (i + 2 * k) % count) for i in range(count)])


def cross_pipe(value, step, bit):
    sections, count = lax.axis_size("pipe"), lax.axis_size("tx")
    pairs = [
        (p * count + i, (p + step) % sections * count + (i ^ bit))
        for p in range(sections)
        for i in range(count)
    ]
    return lax.ppermute(value, ("pipe", "tx"), pairs)


def block_order(count):
    bits = count.bit_length() - 1
    return [int(format(n, f"0{bits}b")[::-1], 2) if bits else 0 for n in range(count)]


def finish(kept, got, own, step):
    count = lax.axis_size("tx")
    bit = 1
    while 2 * bit < count:
        kept = kept + got.astype(F32)
        half = kept.shape[0] // 2
        kept, gone = kept[:half], kept[half:].astype(BF16)
        bit *= 2
        if 2 * bit < count:
            got = swap(gone, "tx", bit)
    near = cross_pipe(kept + own.astype(F32), step, 0)
    return (near + cross_pipe(gone, step, bit).astype(F32)).astype(BF16)


def gather_body(t, count, loads, *refs):
    operands, _, _, arena, _, copies = split(refs, loads, count, 0)
    begin(copies)
    shape = (3 * count * t, 3 * t)
    row = lax.broadcasted_iota(jnp.int32, shape, 0)
    column = lax.broadcasted_iota(jnp.int32, shape, 1)
    kind, row = row // (count * t), row % (count * t)
    source = kind * t + row % t
    picks = [
        jnp.where((row // t == i) & (column == source), 1.0, 0.0).astype(BF16) for i in range(count)
    ]
    base = arena.shape[0] - 7 * count * t
    for low, size in spans(arena.shape[1]):
        piece = pl.ds(low, size)
        rows = sum(contract(pick, operand[:, piece], NN) for pick, operand in zip(picks, operands))
        arena[pl.ds(base, shape[0]), piece] = rows.astype(BF16)
    end(copies)


def after(value, others):
    return lax.optimization_barrier((value, others))[0]


def gathered(section, saved, grads, shape, loads, table, stored):
    count = lax.axis_size("tx")
    t = section.shape[0]
    own = jnp.concatenate([section, saved, grads])
    bit = count // 2
    blocks, near = {0: own}, None
    if count > 1:
        near = swap(after(own, table), "tx", 1)
    arena = load(shape, loads[:-1], table, stored)
    while bit > 1:
        for i in list(blocks):
            blocks[i ^ bit] = swap(blocks[i], "tx", bit)
        bit //= 2
    if count > 1:
        far = [i for i in blocks if i]
        for i in far:
            blocks[i ^ 1] = swap(after(blocks[i], arena), "tx", 1)
        blocks[1] = near
    arena = load(arena, loads[-1:], table, stored)
    order = block_order(count)
    operands = [blocks[i] for i in order]
    body = functools.partial(gather_body, t, count)
    return call(body, operands, [], [], arena, [], table, stored, VM)[0]


def residency(groups, quiet, slots, first):
    uses = [piece for group in groups for piece in group]

    def next_use(piece, at):
        return next((n for n in range(at, len(uses)) if uses[n] == piece), len(uses))

    begun = [(piece, slot, 0) for slot, piece in enumerate(list(dict.fromkeys(uses))[:first])]
    holds = {slot: None for slot in range(slots)}
    holds.update((slot, piece) for piece, slot, _ in begun)
    loads_at, slot_at, at = [], [], 0
    for step, group in enumerate(groups):
        slot_at.append([next(slot for slot, piece in holds.items() if piece == use) for use in group])
        loads = []
        later = at + len(group)
        for stage in range(len(group)):
            busy = slot_at[-1][stage:]
            while True:
                wanted = next((p for p in uses[later:] if p not in holds.values()), None)
                urgent = step + 1 < len(groups) and wanted in groups[step + 1]
                free = [s for s in holds if s not in busy and s not in [slot for _, slot, _ in loads]]
                if wanted is None or not free or (loads or step in quiet) and not urgent:
                    break
                slot = max(free, key=lambda s: next_use(holds[s], later))
                if next_use(holds[slot], later) <= next_use(wanted, later):
                    break
                loads.append((wanted, slot, stage))
                holds[slot] = wanted
        loads_at.append(loads)
        at += len(group)
    return begun, loads_at, slot_at


def local(section_input, saved_input, out_grad, gate_weight, up_weight, down_weight):
    count, tx = lax.axis_size("ty"), lax.axis_size("tx")
    chips = count // 2
    stored = [jnp.swapaxes(gate_weight[0], 0, 1), jnp.swapaxes(up_weight[0], 0, 1), down_weight[0]]
    units = up_to(stored[0].shape[0], 16)
    if units != stored[0].shape[0]:
        stored = [jnp.pad(w, ((0, units - w.shape[0]), (0, 0))) for w in stored]
    share = up_to(-(-units // count), 16)
    cut = share - share // 2 // 128 * 128
    subs = [(0, cut), (cut, share - cut)] if cut < share else [(0, share)]
    most = 3 * max(rows for _, rows in subs)

    me = lax.axis_index("ty")
    core, chip = me % 2, me // 2

    def share_of(k, mine):
        owner = (chip + k) % chips * 2 + (core if mine else 1 - core)
        return owner * share, jnp.minimum(owner * share, units - share)

    def place(k, mine, sub):
        return (share_of(k, mine)[1] + subs[sub][0]).astype(jnp.int32)

    def pieces(chip_order, core_order):
        return [(k, mine, sub) for k in chip_order for mine in core_order for sub in range(len(subs))]

    steps = [("project", [piece]) for piece in pieces(range(1, chips), (False, True)) + pieces((0,), (False,))]
    middle = len(steps) - len(subs) - 1
    if chips > 1:
        steps[middle : middle + 2] = [("project", steps[middle][1] + steps[middle + 1][1])]
    steps += [("activate", [piece]) for piece in pieces((0,), (True,))]
    near, far = pieces((0,), (False,)), pieces(range(1, chips), (True,))
    steps += [("expand", near[n : n + 1] + far[n : n + 1]) for n in range(max(len(near), len(far)))]
    left = pieces(range(1, chips), (False,))
    last = len(subs)
    steps += [("expand", left[n : min(n + 2, len(left) - last)]) for n in range(0, len(left) - last, 2)]
    steps.append(("end", left[-last:]))
    quiet = [n for n, (kind, group) in enumerate(steps) if kind == "project" and group[0][1] and len(group) == 1]
    begun, loads_at, slot_at = residency([group for _, group in steps], quiet, SLOTS, BEGUN)

    entries = {piece: n for n, piece in enumerate(pieces(range(chips), (False, True)))}
    share_at, within = share_of(0, True)
    table = jnp.stack(
        [place(*piece) for piece in entries]
        + [(share_at - within - at).astype(jnp.int32) for at, _ in subs]
    )

    def request(items):
        loads = [(slot * most, subs[piece[2]][1], entries[piece], stage) for piece, slot, stage in items]
        return loads, table, stored

    tokens = tx * section_input.shape[1]
    shape = (SLOTS * most + 7 * tokens, stored[0].shape[1])
    arena = gathered(section_input[0], saved_input[0], out_grad[0], shape, *request(begun))
    passed, arrived, h, forwarded = {}, {}, {}, chips == 1
    for n, (kind, group) in enumerate(steps):
        slots = [(slot * most, subs[piece[2]][1]) for slot, piece in zip(slot_at[n], group)]
        loads = request(loads_at[n])
        if kind in ("project", "activate"):
            jobs = []
            for slot, (k, mine, sub) in zip(slots, group):
                more = passed.pop((k, sub)) if mine else []
                if mine and not k:
                    jobs.append((slot, more, arrived.get(sub, []), (), F32, len(entries) + sub, not sub))
                else:
                    leave, dtype = ((5,), BF16) if mine else ((5,) if k else SPLIT, F32)
                    jobs.append((slot, more, [], leave, dtype, None, False))
            parts, arena = project(tokens, arena, jobs, *loads)
            for k, mine, sub in group:
                if mine and not k:
                    own = parts.pop(0)
                    h[0, True, sub] = own
                    for i in range(1, chips):
                        h[i, True, sub] = to_chip(own, chips - i)
                    h[0, False, sub] = swap(own, "ty", 1)
                elif mine:
                    arrived.setdefault(sub, []).append(to_chip(parts.pop(0), k))
                else:
                    count = 1 if k else len(SPLIT)
                    passed[k, sub] = [swap(parts.pop(0), "ty", 1) for _ in range(count)]
        elif kind == "expand":
            held = [h[piece] for piece in group]
            _, arena = expand(tokens, held, arena, slots, (0, 1), False, *loads)
            if not forwarded and len(h) == len(subs) * (chips + 1):
                forwarded = True
                for i in range(1, chips):
                    for j in range(len(subs)):
                        h[i, False, j] = swap(after(h[i, True, j], arena), "ty", 1)
        else:
            if not forwarded:
                for i in range(1, chips):
                    for j in range(len(subs)):
                        h[i, False, j] = swap(h[i, True, j], "ty", 1)
            held = [h[piece] for piece in group]
            (kept, gone), arena = expand(tokens, held, arena, slots, (0,), True, *loads)
            got = swap(gone, "tx", 1)
            (kept_back, gone), _ = expand(tokens, held, arena, slots, (1,), True, *request([]))
            next_input = finish(kept, got, section_input[0], 1)
            prev_grad = finish(kept_back, swap(gone, "tx", 1), out_grad[0], -1)
    return (next_input[None], prev_grad[None])


def solution(mesh):
    return jax.shard_map(
        local,
        mesh=mesh,
        in_specs=(
            P("pipe", "tx", "ty"),
            P("pipe", "tx", "ty"),
            P("pipe", "tx", "ty"),
            P("pipe", "ty", "tx"),
            P("pipe", "ty", "tx"),
            P("pipe", "tx", "ty"),
        ),
        out_specs=(P("pipe", "tx", "ty"), P("pipe", "tx", "ty")),
        check_vma=False,
    )
```

```python
import functools

import jax
import jax.numpy as jnp
from jax import lax
from jax.experimental import pallas as pl
from jax.experimental.pallas import tpu as pltpu
from jax.sharding import PartitionSpec as P

F32 = jnp.float32
BF16 = jnp.bfloat16
NN = (((1,), (0,)), ((), ()))
NT = (((1,), (1,)), ((), ()))
VM = pl.BlockSpec(memory_space=pltpu.VMEM)
HBM = pl.BlockSpec(memory_space=pltpu.HBM)
SM = pl.BlockSpec(memory_space=pltpu.SMEM)
STEP = 384
SLOTS = 5
BEGUN = 2
SPLIT = (2, 2, 1)
HINT = 2 * 10**9


def contract(a, b, dims):
    return lax.dot_general(a, b, dims, preferred_element_type=F32)


def params():
    return pltpu.CompilerParams(vmem_limit_bytes=62 * 2**20 // 10)


def spans(size, step=STEP):
    return [(at, min(step, size - at)) for at in range(0, size, step)]


def up_to(value, unit):
    return -(-value // unit) * unit


def fetches(table_ref, stored, arena, loads, sems):
    copies = []
    for n, (at, rows, entry, _) in enumerate(loads):
        start = pl.multiple_of(table_ref[entry], 16)
        for i, source in enumerate(stored):
            target = arena.at[pl.ds(at + i * rows, rows), :]
            copies.append(pltpu.make_async_copy(source.at[pl.ds(start, rows), :], target, sems.at[n, i]))
    return copies


def begin(copies):
    for copy in copies:
        copy.start()


def end(copies):
    for copy in copies:
        copy.wait()


def call(body, operands, shapes, scratch, arena, loads, table, stored, spec=HBM, weight=1):
    operands, specs = [*operands, table], [spec] * len(operands) + [SM]
    aliases, scratch = {}, list(scratch)
    if loads:
        operands += stored
        specs += [HBM] * 3
        scratch.append(pltpu.SemaphoreType.DMA((len(loads), 3)))
    held = []
    if isinstance(arena, tuple):
        held = [pltpu.VMEM(arena, BF16)]
    elif arena is not None:
        held = [pltpu.VMEM(arena.shape, BF16)]
        aliases = {len(operands): len(shapes)}
        operands.append(arena)
        specs.append(VM)
    return pl.pallas_call(
        functools.partial(body, loads),
        in_specs=specs,
        out_specs=[spec] * len(shapes) + [VM] * len(held),
        out_shape=list(shapes) + held,
        scratch_shapes=scratch,
        input_output_aliases=aliases,
        compiler_params=params(),
        cost_estimate=pl.CostEstimate(flops=weight * HINT, bytes_accessed=0, transcendentals=0),
    )(*operands)


def split(refs, loads, count, outs, carried=True):
    operands, table, refs = refs[:count], refs[count], refs[count + 1 :]
    if loads:
        stored, refs = refs[:3], refs[3:]
    if carried:
        refs = refs[1:]
    results, arena, scratch = refs[:outs], refs[outs], refs[outs + 1 :]
    if carried is None:
        arena, scratch = None, refs[outs:]
    copies = []
    if loads:
        copies, scratch = fetches(table, stored, arena, loads, scratch[-1]), scratch[:-1]
    return operands, table, results, arena, scratch, copies


def load_body(carried, loads, *refs):
    copies = split(refs, loads, 0, 0, carried)[-1]
    begin(copies)
    end(copies)


def load(arena, loads, table, stored):
    carried = not isinstance(arena, tuple)
    return call(functools.partial(load_body, carried), [], [], [], arena, loads, table, stored)[0]


def products(arena, h_refs, slots, part, tokens, piece):
    value = 0.0
    for h_ref, (at, rows) in zip(h_refs, slots):
        for i in (1, 2) if part else (0,):
            lhs = h_ref[pl.ds(i * tokens, tokens), :]
            value = value + contract(lhs, arena[pl.ds(at + (i + 2) % 3 * rows, rows), piece], NN)
    return value


def sum_rows(arena, part, tokens):
    low = arena.shape[0] - 4 * tokens + 2 * part * tokens
    return pl.ds(low, tokens), pl.ds(low + tokens, tokens)


def keep(arena, value, part, tokens, piece):
    high, low = sum_rows(arena, part, tokens)
    rounded = value.astype(BF16)
    arena[high, piece] = rounded
    arena[low, piece] = (value - rounded.astype(F32)).astype(BF16)


def kept_sum(arena, part, tokens, piece):
    high, low = sum_rows(arena, part, tokens)
    return arena[high, piece].astype(F32) + arena[low, piece].astype(F32)


def project_body(jobs, tokens, loads, *refs):
    ins = sum(len(job["got"]) + job["others"] for job in jobs)
    outs = sum(len(job["leave"]) or 1 for job in jobs)
    operands, table, out_refs, arena, scratch, copies = split(refs, loads, ins, outs)
    operands, out_refs, scratch = list(operands), list(out_refs), list(scratch)
    blocks = [pl.ds(0, 2 * tokens), pl.ds(2 * tokens, 2 * tokens), pl.ds(4 * tokens, tokens)]
    base = arena.shape[0] - 7 * tokens
    work = []
    for job in jobs:
        part_ref, out_sems = scratch.pop(0), scratch.pop(0)
        held = [scratch.pop(0) for _ in range(job["others"] + bool(job["got"]))]
        targets, low = [], 0
        for count in job["got"]:
            targets.append(held[0].at[pl.ds(low, count * tokens), :])
            low += count * tokens
        targets += held[bool(job["got"]) :]
        in_sems = scratch.pop(0) if targets else None
        arrivals = [
            pltpu.make_async_copy(operands.pop(0), target, in_sems.at[i]) for i, target in enumerate(targets)
        ]
        begin(arrivals)
        h_ref = scratch.pop(0) if job["entry"] is not None else None
        first_ref = part_ref
        if targets and h_ref is None:
            first_ref = scratch.pop(0)
        to = [out_refs.pop(0) for _ in range(len(job["leave"]) or 1)]
        work.append((job, part_ref, out_sems, held, arrivals, h_ref, first_ref, to))
    if not work[0][4]:
        begin(copies)
    leaving = []

    for number, (job, part_ref, out_sems, held, arrivals, h_ref, first_ref, to) in enumerate(work):
        at, rows, entry = job["at"], job["rows"], job["entry"]
        pending = (0, 1, 2) if copies and entry is None and len(work) == 1 else (0,)
        pending = pending if arrivals else ()
        if arrivals and pending == (0, 1, 2) and not number:
            begin(copies)

        def finished(part, i, piece):
            for ref in held:
                part = part + ref[blocks[i], piece].astype(F32)
            return part

        def complete(i):
            for low, size in spans(rows):
                piece = pl.ds(low, size)
                part = finished(first_ref[blocks[i], piece], i, piece)
                part_ref[blocks[i], piece] = part.astype(part_ref.dtype)

        def leaves(i):
            if entry is None:
                target = to[0].at[blocks[i], :] if len(to) == 1 else to[i]
                leaving.append(pltpu.make_async_copy(part_ref.at[blocks[i], :], target, out_sems.at[i]))
                leaving[-1].start()

        for i, (first, count) in enumerate(((0, 2), (0, 2), (2, 1))):
            lhs = arena[pl.ds(base + first * tokens, count * tokens), :]
            for low, size in spans(rows):
                piece = pl.ds(low, size)
                part = contract(lhs, arena[pl.ds(at + i * rows + low, size), :], NT)
                if i in pending:
                    first_ref[blocks[i], piece] = part
                    continue
                if pending and i == 1 and not low:
                    end(arrivals)
                    if not number:
                        begin(copies)
                part_ref[blocks[i], piece] = finished(part, i, piece).astype(part_ref.dtype)
                if i < 2 or entry is None:
                    continue
                for at_column in range(low, low + size, 128):
                    columns = pl.ds(at_column, min(128, low + size - at_column))
                    gate, saved_gate, up, saved_up, hidden_grad = [
                        part_ref[pl.ds(n * tokens, tokens), columns] for n in range(5)
                    ]
                    mine = lax.broadcasted_iota(jnp.int32, gate.shape, 1) + at_column >= table[entry]
                    hidden = gate * jax.nn.sigmoid(gate) * up
                    sigma = jax.nn.sigmoid(saved_gate)
                    gate_grad = hidden_grad * saved_up * sigma * (1.0 + saved_gate * (1.0 - sigma))
                    up_grad = hidden_grad * saved_gate * sigma
                    for n, value in enumerate((hidden, gate_grad, up_grad)):
                        h_ref[pl.ds(n * tokens, tokens), columns] = jnp.where(mine, value, 0.0).astype(BF16)
            if i == 1 and pending == (0,):
                complete(0)
                leaves(0)
            if i not in pending:
                leaves(i)
        if pending == (0, 1, 2):
            end(arrivals)
            for i in pending:
                complete(i)
                leaves(i)
        if entry is not None:
            leaving.append(pltpu.make_async_copy(h_ref, to[0], out_sems.at[0]))
            leaving[-1].start()
            for low, size in spans(arena.shape[1]):
                piece = pl.ds(low, size)
                for part in (0, 1):
                    value = products(arena, [h_ref], [(at, rows)], part, tokens, piece)
                    if not job["fresh"]:
                        value = value + kept_sum(arena, part, tokens, piece)
                    keep(arena, value, part, tokens, piece)
    end(leaving)
    end(copies)


def project(tokens, arena, jobs, loads, table, stored):
    operands, shapes, scratch, static = [], [], [], []
    for (at, rows), more, others, leave, dtype, entry, fresh in jobs:
        operands += more + others
        part = jax.ShapeDtypeStruct((5 * tokens, rows), dtype)
        scratch += [pltpu.VMEM(part.shape, dtype), pltpu.SemaphoreType.DMA((3,))]
        scratch += [pltpu.VMEM(part.shape, F32)] * (1 if more else 0)
        scratch += [pltpu.VMEM(operand.shape, operand.dtype) for operand in others]
        if more or others:
            scratch.append(pltpu.SemaphoreType.DMA((len(more + others),)))
        if entry is not None:
            shapes.append(jax.ShapeDtypeStruct((3 * tokens, rows), BF16))
            scratch.append(pltpu.VMEM(shapes[-1].shape, BF16))
        else:
            shapes += [jax.ShapeDtypeStruct((count * tokens, rows), dtype) for count in leave]
            if more or others:
                scratch.append(pltpu.VMEM(part.shape, F32))
        got = [piece.shape[0] // tokens for piece in more]
        static.append(dict(at=at, rows=rows, got=got, others=len(others), leave=leave, entry=entry, fresh=fresh))
    weight = sum(1 if job["entry"] is None else 6 for job in static)
    body = functools.partial(project_body, static, tokens)
    *outs, arena = call(body, operands, shapes, scratch, arena, loads, table, stored, weight=weight)
    return outs, arena


def expand_body(slots, devices, tokens, loads, *refs):
    operands, _, outs, arena, scratch, copies = split(refs, loads, len(slots), 2 if devices else 0)
    in_sems, *held = scratch
    arrivals = [pltpu.make_async_copy(operand, held[i], in_sems.at[i]) for i, operand in enumerate(operands)]
    begin(arrivals)
    leaving = []
    if devices:
        out_sems, total_ref, gone_ref = held[len(slots) :]
        t = tokens // devices
    for n, slot in enumerate(slots):
        if not n and len(slots) > 1:
            end(arrivals)
        for i, copy in enumerate(copies):
            if loads[i // 3][3] == n:
                copy.start()
        if not n and len(slots) == 1:
            end(arrivals)
        for m, (low, size) in enumerate(spans(arena.shape[1])):
            piece = pl.ds(low, size)
            for part in (0, 1):
                value = products(arena, [held[n]], [slot], part, tokens, piece)
                value = value + kept_sum(arena, part, tokens, piece)
                if not devices or n < len(slots) - 1:
                    keep(arena, value, part, tokens, piece)
                    continue
                for i in range(devices):
                    total_ref[pl.ds((2 * i + part) * t, t), piece] = value[i * t : (i + 1) * t]
            if devices and n == len(slots) - 1:
                gone_ref[:, piece] = total_ref[pl.ds(tokens, tokens), piece].astype(BF16)
                for k, source in enumerate((total_ref.at[pl.ds(0, tokens), piece], gone_ref.at[:, piece])):
                    copy = pltpu.make_async_copy(source, outs[k].at[:, piece], out_sems.at[k, m])
                    leaving.append(copy)
                    copy.start()
    end(leaving)
    end(copies)


def expand(tokens, held, arena, slots, devices, loads, table, stored):
    width = arena.shape[1]
    shapes = []
    scratch = [pltpu.SemaphoreType.DMA((len(held),))]
    scratch += [pltpu.VMEM(operand.shape, operand.dtype) for operand in held]
    if devices:
        shapes = [jax.ShapeDtypeStruct((tokens, width), dtype) for dtype in (F32, BF16)]
        scratch.append(pltpu.SemaphoreType.DMA((2, len(spans(width)))))
        scratch += [pltpu.VMEM((2 * tokens, width), F32), pltpu.VMEM((tokens, width), BF16)]
    body = functools.partial(expand_body, slots, devices, tokens)
    *outs, arena = call(body, held, shapes, scratch, arena, loads, table, stored)
    return outs, arena


def swap(value, axis, bit):
    return lax.ppermute(value, axis, [(i, i ^ bit) for i in range(lax.axis_size(axis))])


def to_chip(value, k):
    count = lax.axis_size("ty")
    return lax.ppermute(value, "ty", [(i, (i + 2 * k) % count) for i in range(count)])


def cross_pipe(value, step, bit):
    sections, count = lax.axis_size("pipe"), lax.axis_size("tx")
    pairs = [
        (p * count + i, (p + step) % sections * count + (i ^ bit))
        for p in range(sections)
        for i in range(count)
    ]
    return lax.ppermute(value, ("pipe", "tx"), pairs)


def block_order(count):
    bits = count.bit_length() - 1
    return [int(format(n, f"0{bits}b")[::-1], 2) if bits else 0 for n in range(count)]


def finish(kept, got, t, ahead, back):
    count = lax.axis_size("tx")

    def across(value, bit):
        if lax.axis_size("pipe") == 2:
            return cross_pipe(value, 1, bit)
        return jnp.concatenate([cross_pipe(value[:t], 1, bit), cross_pipe(value[t:], -1, bit)])

    bit = 1
    while 2 * bit < count:
        kept = kept + got.astype(F32)
        half = kept.shape[0] // 2
        kept, gone = kept[:half], kept[half:].astype(BF16)
        bit *= 2
        if 2 * bit < count:
            got = swap(gone, "tx", bit)
    far = across(gone, bit)
    near = across(kept.astype(BF16), 0)
    total = near.astype(F32) + far.astype(F32)
    return (total[:t] + ahead.astype(F32)).astype(BF16), (total[t:] + back.astype(F32)).astype(BF16)


def gather_body(t, count, loads, *refs):
    operands, _, _, arena, _, copies = split(refs, loads, count, 0)
    begin(copies)
    shape = (3 * count * t, 3 * t)
    row = lax.broadcasted_iota(jnp.int32, shape, 0)
    column = lax.broadcasted_iota(jnp.int32, shape, 1)
    kind, row = row // (count * t), row % (count * t)
    source = kind * t + row % t
    picks = [
        jnp.where((row // t == i) & (column == source), 1.0, 0.0).astype(BF16) for i in range(count)
    ]
    base = arena.shape[0] - 7 * count * t
    for low, size in spans(arena.shape[1]):
        piece = pl.ds(low, size)
        rows = sum(contract(pick, operand[:, piece], NN) for pick, operand in zip(picks, operands))
        arena[pl.ds(base, shape[0]), piece] = rows.astype(BF16)
    end(copies)


def after(value, others):
    return lax.optimization_barrier((value, others))[0]


def gathered(section, saved, grads, shape, loads, table, stored):
    count = lax.axis_size("tx")
    t = section.shape[0]
    own = jnp.concatenate([section, saved, grads])
    bit = count // 2
    blocks, near = {0: own}, None
    if count > 1:
        near = swap(after(own, table), "tx", 1)
    arena = load(shape, loads[:-1], table, stored)
    later = after(own, arena)
    ahead = cross_pipe(later, 1, 0)
    back = ahead if lax.axis_size("pipe") == 2 else cross_pipe(later, -1, 0)
    while bit > 1:
        for i in list(blocks):
            blocks[i ^ bit] = swap(blocks[i], "tx", bit)
        bit //= 2
    if count > 1:
        far = [i for i in blocks if i]
        for i in far:
            blocks[i ^ 1] = swap(after(blocks[i], arena), "tx", 1)
        blocks[1] = near
    arena = load(arena, loads[-1:], table, stored)
    order = block_order(count)
    operands = [blocks[i] for i in order]
    body = functools.partial(gather_body, t, count)
    arena = call(body, operands, [], [], after(arena, (ahead, back)), [], table, stored, VM)[0]
    return arena, ahead[:t], back[2 * t :]


def residency(groups, quiet, slots, first):
    uses = [piece for group in groups for piece in group]

    def next_use(piece, at):
        return next((n for n in range(at, len(uses)) if uses[n] == piece), len(uses))

    begun = [(piece, slot, 0) for slot, piece in enumerate(list(dict.fromkeys(uses))[:first])]
    holds = {slot: None for slot in range(slots)}
    holds.update((slot, piece) for piece, slot, _ in begun)
    loads_at, slot_at, at = [], [], 0
    for step, group in enumerate(groups):
        slot_at.append([next(slot for slot, piece in holds.items() if piece == use) for use in group])
        loads = []
        later = at + len(group)
        for stage in range(len(group)):
            busy = slot_at[-1][stage:]
            while True:
                wanted = next((p for p in uses[later:] if p not in holds.values()), None)
                urgent = step + 1 < len(groups) and wanted in groups[step + 1]
                free = [s for s in holds if s not in busy and s not in [slot for _, slot, _ in loads]]
                if wanted is None or not free or (loads or step in quiet) and not urgent:
                    break
                slot = max(free, key=lambda s: next_use(holds[s], later))
                if next_use(holds[slot], later) <= next_use(wanted, later):
                    break
                loads.append((wanted, slot, stage))
                holds[slot] = wanted
        loads_at.append(loads)
        at += len(group)
    return begun, loads_at, slot_at


def local(section_input, saved_input, out_grad, gate_weight, up_weight, down_weight):
    count, tx = lax.axis_size("ty"), lax.axis_size("tx")
    chips = count // 2
    stored = [jnp.swapaxes(gate_weight[0], 0, 1), jnp.swapaxes(up_weight[0], 0, 1), down_weight[0]]
    units = up_to(stored[0].shape[0], 16)
    if units != stored[0].shape[0]:
        stored = [jnp.pad(w, ((0, units - w.shape[0]), (0, 0))) for w in stored]
    share = up_to(-(-units // count), 16)
    cut = share - share // 2 // 128 * 128
    subs = [(0, cut), (cut, share - cut)] if cut < share else [(0, share)]
    most = 3 * max(rows for _, rows in subs)

    me = lax.axis_index("ty")
    core, chip = me % 2, me // 2

    def share_of(k, mine):
        owner = (chip + k) % chips * 2 + (core if mine else 1 - core)
        return owner * share, jnp.minimum(owner * share, units - share)

    def place(k, mine, sub):
        return (share_of(k, mine)[1] + subs[sub][0]).astype(jnp.int32)

    def pieces(chip_order, core_order):
        return [(k, mine, sub) for k in chip_order for mine in core_order for sub in range(len(subs))]

    steps = [("project", [piece]) for piece in pieces(range(1, chips), (False, True)) + pieces((0,), (False,))]
    middle = len(steps) - len(subs) - 1
    if chips > 1:
        steps[middle : middle + 2] = [("project", steps[middle][1] + steps[middle + 1][1])]
    steps += [("activate", [piece]) for piece in pieces((0,), (True,))]
    near, far = pieces((0,), (False,)), pieces(range(1, chips), (True,))
    steps += [("expand", near[n : n + 1] + far[n : n + 1]) for n in range(max(len(near), len(far)))]
    left = pieces(range(1, chips), (False,))
    last = len(subs)
    steps += [("expand", left[n : min(n + 2, len(left) - last)]) for n in range(0, len(left) - last, 2)]
    steps.append(("end", left[-last:]))
    quiet = [n for n, (kind, group) in enumerate(steps) if kind == "project" and group[0][1] and len(group) == 1]
    begun, loads_at, slot_at = residency([group for _, group in steps], quiet, SLOTS, BEGUN)

    entries = {piece: n for n, piece in enumerate(pieces(range(chips), (False, True)))}
    share_at, within = share_of(0, True)
    table = jnp.stack(
        [place(*piece) for piece in entries]
        + [(share_at - within - at).astype(jnp.int32) for at, _ in subs]
    )

    def request(items):
        loads = [(slot * most, subs[piece[2]][1], entries[piece], stage) for piece, slot, stage in items]
        return loads, table, stored

    tokens = tx * section_input.shape[1]
    shape = (SLOTS * most + 7 * tokens, stored[0].shape[1])
    arena, ahead, back = gathered(section_input[0], saved_input[0], out_grad[0], shape, *request(begun))
    passed, arrived, h, forwarded = {}, {}, {}, chips == 1
    for n, (kind, group) in enumerate(steps):
        slots = [(slot * most, subs[piece[2]][1]) for slot, piece in zip(slot_at[n], group)]
        loads = request(loads_at[n])
        if kind in ("project", "activate"):
            jobs = []
            for slot, (k, mine, sub) in zip(slots, group):
                more = passed.pop((k, sub)) if mine else []
                if mine and not k:
                    jobs.append((slot, more, arrived.get(sub, []), (), F32, len(entries) + sub, not sub))
                else:
                    leave, dtype = ((5,), BF16) if mine else ((5,) if k or sub else SPLIT, F32)
                    jobs.append((slot, more, [], leave, dtype, None, False))
            parts, arena = project(tokens, arena, jobs, *loads)
            for k, mine, sub in group:
                if mine and not k:
                    own = parts.pop(0)
                    h[0, True, sub] = own
                    for i in range(1, chips):
                        h[i, True, sub] = to_chip(own, chips - i)
                    h[0, False, sub] = swap(own, "ty", 1)
                elif mine:
                    arrived.setdefault(sub, []).append(to_chip(parts.pop(0), k))
                else:
                    count = 1 if k or sub else len(SPLIT)
                    passed[k, sub] = [swap(parts.pop(0), "ty", 1) for _ in range(count)]
        elif kind == "expand":
            held = [h[piece] for piece in group]
            _, arena = expand(tokens, held, arena, slots, 0, *loads)
            if not forwarded and len(h) == len(subs) * (chips + 1):
                forwarded = True
                for i in range(1, chips):
                    for j in range(len(subs)):
                        h[i, False, j] = swap(after(h[i, True, j], arena), "ty", 1)
        else:
            if not forwarded:
                for i in range(1, chips):
                    for j in range(len(subs)):
                        h[i, False, j] = swap(h[i, True, j], "ty", 1)
            held = [h[piece] for piece in group]
            (kept, gone), _ = expand(tokens, held, arena, slots, tx, *loads)
            got = swap(gone, "tx", 1)
            next_input, prev_grad = finish(kept, got, section_input.shape[1], ahead, back)
    return (next_input[None], prev_grad[None])


def solution(mesh):
    return jax.shard_map(
        local,
        mesh=mesh,
        in_specs=(
            P("pipe", "tx", "ty"),
            P("pipe", "tx", "ty"),
            P("pipe", "tx", "ty"),
            P("pipe", "ty", "tx"),
            P("pipe", "ty", "tx"),
            P("pipe", "tx", "ty"),
        ),
        out_specs=(P("pipe", "tx", "ty"), P("pipe", "tx", "ty")),
        check_vma=False,
    )
```

```python
import functools

import jax
import jax.numpy as jnp
from jax import lax
from jax.experimental import pallas as pl
from jax.experimental.pallas import tpu as pltpu
from jax.sharding import PartitionSpec as P

F32 = jnp.float32
BF16 = jnp.bfloat16
NN = (((1,), (0,)), ((), ()))
NT = (((1,), (1,)), ((), ()))
VM = pl.BlockSpec(memory_space=pltpu.VMEM)
HBM = pl.BlockSpec(memory_space=pltpu.HBM)
SM = pl.BlockSpec(memory_space=pltpu.SMEM)
STEP = 384
SLOTS = 5
BEGUN = 2
SPLIT = (2, 2, 1)
HINT = 2 * 10**9


def contract(a, b, dims):
    return lax.dot_general(a, b, dims, preferred_element_type=F32)


def params():
    return pltpu.CompilerParams(vmem_limit_bytes=62 * 2**20 // 10)


def spans(size, step=STEP):
    return [(at, min(step, size - at)) for at in range(0, size, step)]


def up_to(value, unit):
    return -(-value // unit) * unit


def fetches(table_ref, stored, arena, loads, sems):
    copies = []
    for n, (at, rows, entry, _) in enumerate(loads):
        start = pl.multiple_of(table_ref[entry], 16)
        for i, source in enumerate(stored):
            target = arena.at[pl.ds(at + i * rows, rows), :]
            copies.append(pltpu.make_async_copy(source.at[pl.ds(start, rows), :], target, sems.at[n, i]))
    return copies


def begin(copies):
    for copy in copies:
        copy.start()


def end(copies):
    for copy in copies:
        copy.wait()


def call(body, operands, shapes, scratch, arena, loads, table, stored, spec=HBM, weight=1):
    operands, specs = [*operands, table], [spec] * len(operands) + [SM]
    aliases, scratch = {}, list(scratch)
    if loads:
        operands += stored
        specs += [HBM] * 3
        scratch.append(pltpu.SemaphoreType.DMA((len(loads), 3)))
    held = []
    if isinstance(arena, tuple):
        held = [pltpu.VMEM(arena, BF16)]
    elif arena is not None:
        held = [pltpu.VMEM(arena.shape, BF16)]
        aliases = {len(operands): len(shapes)}
        operands.append(arena)
        specs.append(VM)
    return pl.pallas_call(
        functools.partial(body, loads),
        in_specs=specs,
        out_specs=[spec] * len(shapes) + [VM] * len(held),
        out_shape=list(shapes) + held,
        scratch_shapes=scratch,
        input_output_aliases=aliases,
        compiler_params=params(),
        cost_estimate=pl.CostEstimate(flops=weight * HINT, bytes_accessed=0, transcendentals=0),
    )(*operands)


def split(refs, loads, count, outs, carried=True):
    operands, table, refs = refs[:count], refs[count], refs[count + 1 :]
    if loads:
        stored, refs = refs[:3], refs[3:]
    if carried:
        refs = refs[1:]
    results, arena, scratch = refs[:outs], refs[outs], refs[outs + 1 :]
    if carried is None:
        arena, scratch = None, refs[outs:]
    copies = []
    if loads:
        copies, scratch = fetches(table, stored, arena, loads, scratch[-1]), scratch[:-1]
    return operands, table, results, arena, scratch, copies


def load_body(carried, loads, *refs):
    copies = split(refs, loads, 0, 0, carried)[-1]
    begin(copies)
    end(copies)


def load(arena, loads, table, stored):
    carried = not isinstance(arena, tuple)
    return call(functools.partial(load_body, carried), [], [], [], arena, loads, table, stored)[0]


def products(arena, h_refs, slots, part, tokens, piece):
    value = 0.0
    for h_ref, (at, rows) in zip(h_refs, slots):
        for i in (1, 2) if part else (0,):
            lhs = h_ref[pl.ds(i * tokens, tokens), :]
            value = value + contract(lhs, arena[pl.ds(at + (i + 2) % 3 * rows, rows), piece], NN)
    return value


def sum_rows(arena, part, tokens):
    low = arena.shape[0] - 4 * tokens + 2 * part * tokens
    return pl.ds(low, tokens), pl.ds(low + tokens, tokens)


def keep(arena, value, part, tokens, piece):
    high, low = sum_rows(arena, part, tokens)
    rounded = value.astype(BF16)
    arena[high, piece] = rounded
    arena[low, piece] = (value - rounded.astype(F32)).astype(BF16)


def kept_sum(arena, part, tokens, piece):
    high, low = sum_rows(arena, part, tokens)
    return arena[high, piece].astype(F32) + arena[low, piece].astype(F32)


def project_body(jobs, tokens, loads, *refs):
    ins = sum(len(job["got"]) + job["others"] for job in jobs)
    outs = sum(len(job["leave"]) or 1 for job in jobs)
    operands, table, out_refs, arena, scratch, copies = split(refs, loads, ins, outs)
    operands, out_refs, scratch = list(operands), list(out_refs), list(scratch)
    blocks = [pl.ds(0, 2 * tokens), pl.ds(2 * tokens, 2 * tokens), pl.ds(4 * tokens, tokens)]
    base = arena.shape[0] - 7 * tokens
    work = []
    for job in jobs:
        part_ref, out_sems = scratch.pop(0), scratch.pop(0)
        held = [scratch.pop(0) for _ in range(job["others"] + bool(job["got"]))]
        targets, low = [], 0
        for count in job["got"]:
            targets.append(held[0].at[pl.ds(low, count * tokens), :])
            low += count * tokens
        targets += held[bool(job["got"]) :]
        in_sems = scratch.pop(0) if targets else None
        arrivals = [
            pltpu.make_async_copy(operands.pop(0), target, in_sems.at[i]) for i, target in enumerate(targets)
        ]
        begin(arrivals)
        h_ref = scratch.pop(0) if job["entry"] is not None else None
        first_ref = part_ref
        if targets and h_ref is None:
            first_ref = scratch.pop(0)
        to = [out_refs.pop(0) for _ in range(len(job["leave"]) or 1)]
        work.append((job, part_ref, out_sems, held, arrivals, h_ref, first_ref, to))
    if not work[0][4]:
        begin(copies)
    leaving = []

    for number, (job, part_ref, out_sems, held, arrivals, h_ref, first_ref, to) in enumerate(work):
        at, rows, entry = job["at"], job["rows"], job["entry"]
        step = 512 if job["fresh"] else STEP
        pending = (0, 1, 2) if copies and entry is None and len(work) == 1 else (0,)
        pending = pending if arrivals else ()
        if arrivals and pending == (0, 1, 2) and not number:
            begin(copies)

        def finished(part, i, piece):
            for ref in held:
                part = part + ref[blocks[i], piece].astype(F32)
            return part

        def complete(i):
            for low, size in spans(rows, step):
                piece = pl.ds(low, size)
                part = finished(first_ref[blocks[i], piece], i, piece)
                part_ref[blocks[i], piece] = part.astype(part_ref.dtype)

        def leaves(i):
            if entry is None:
                target = to[0].at[blocks[i], :] if len(to) == 1 else to[i]
                leaving.append(pltpu.make_async_copy(part_ref.at[blocks[i], :], target, out_sems.at[i]))
                leaving[-1].start()

        for i, (first, count) in enumerate(((0, 2), (0, 2), (2, 1))):
            lhs = arena[pl.ds(base + first * tokens, count * tokens), :]
            for low, size in spans(rows, step):
                piece = pl.ds(low, size)
                part = contract(lhs, arena[pl.ds(at + i * rows + low, size), :], NT)
                if i in pending:
                    first_ref[blocks[i], piece] = part
                    continue
                if pending and i == 1 and not low:
                    end(arrivals)
                    if not number:
                        begin(copies)
                part_ref[blocks[i], piece] = finished(part, i, piece).astype(part_ref.dtype)
                if i < 2 or entry is None:
                    continue
                for at_column in range(low, low + size, 128):
                    columns = pl.ds(at_column, min(128, low + size - at_column))
                    gate, saved_gate, up, saved_up, hidden_grad = [
                        part_ref[pl.ds(n * tokens, tokens), columns] for n in range(5)
                    ]
                    mine = lax.broadcasted_iota(jnp.int32, gate.shape, 1) + at_column >= table[entry]
                    hidden = gate * jax.nn.sigmoid(gate) * up
                    sigma = jax.nn.sigmoid(saved_gate)
                    gate_grad = hidden_grad * saved_up * sigma * (1.0 + saved_gate * (1.0 - sigma))
                    up_grad = hidden_grad * saved_gate * sigma
                    for n, value in enumerate((hidden, gate_grad, up_grad)):
                        h_ref[pl.ds(n * tokens, tokens), columns] = jnp.where(mine, value, 0.0).astype(BF16)
            if i == 1 and pending == (0,):
                complete(0)
                leaves(0)
            if i not in pending:
                leaves(i)
        if pending == (0, 1, 2):
            end(arrivals)
            for i in pending:
                complete(i)
                leaves(i)
        if entry is not None:
            leaving.append(pltpu.make_async_copy(h_ref, to[0], out_sems.at[0]))
            leaving[-1].start()
            for low, size in spans(arena.shape[1], step):
                piece = pl.ds(low, size)
                for part in (0, 1):
                    value = products(arena, [h_ref], [(at, rows)], part, tokens, piece)
                    if not job["fresh"]:
                        value = value + kept_sum(arena, part, tokens, piece)
                    keep(arena, value, part, tokens, piece)
    end(leaving)
    end(copies)


def project(tokens, arena, jobs, loads, table, stored):
    operands, shapes, scratch, static = [], [], [], []
    for (at, rows), more, others, leave, dtype, entry, fresh in jobs:
        operands += more + others
        part = jax.ShapeDtypeStruct((5 * tokens, rows), dtype)
        scratch += [pltpu.VMEM(part.shape, dtype), pltpu.SemaphoreType.DMA((3,))]
        scratch += [pltpu.VMEM(part.shape, F32)] * (1 if more else 0)
        scratch += [pltpu.VMEM(operand.shape, operand.dtype) for operand in others]
        if more or others:
            scratch.append(pltpu.SemaphoreType.DMA((len(more + others),)))
        if entry is not None:
            shapes.append(jax.ShapeDtypeStruct((3 * tokens, rows), BF16))
            scratch.append(pltpu.VMEM(shapes[-1].shape, BF16))
        else:
            shapes += [jax.ShapeDtypeStruct((count * tokens, rows), dtype) for count in leave]
            if more or others:
                scratch.append(pltpu.VMEM(part.shape, F32))
        got = [piece.shape[0] // tokens for piece in more]
        static.append(dict(at=at, rows=rows, got=got, others=len(others), leave=leave, entry=entry, fresh=fresh))
    weight = sum(1 if job["entry"] is None else 6 for job in static)
    body = functools.partial(project_body, static, tokens)
    *outs, arena = call(body, operands, shapes, scratch, arena, loads, table, stored, weight=weight)
    return outs, arena


def expand_body(slots, devices, tokens, loads, *refs):
    operands, _, outs, arena, scratch, copies = split(refs, loads, len(slots), 2 if devices else 0)
    in_sems, *held = scratch
    arrivals = [pltpu.make_async_copy(operand, held[i], in_sems.at[i]) for i, operand in enumerate(operands)]
    begin(arrivals)
    leaving = []
    if devices:
        out_sems, total_ref, gone_ref = held[len(slots) :]
        t = tokens // devices
    for n, slot in enumerate(slots):
        if not n and len(slots) > 1:
            end(arrivals)
        for i, copy in enumerate(copies):
            if loads[i // 3][3] == n:
                copy.start()
        if not n and len(slots) == 1:
            end(arrivals)
        for m, (low, size) in enumerate(spans(arena.shape[1])):
            piece = pl.ds(low, size)
            for part in (0, 1):
                value = products(arena, [held[n]], [slot], part, tokens, piece)
                value = value + kept_sum(arena, part, tokens, piece)
                if not devices or n < len(slots) - 1:
                    keep(arena, value, part, tokens, piece)
                    continue
                for i in range(devices):
                    total_ref[pl.ds((2 * i + part) * t, t), piece] = value[i * t : (i + 1) * t]
            if devices and n == len(slots) - 1:
                gone_ref[:, piece] = total_ref[pl.ds(tokens, tokens), piece].astype(BF16)
                for k, source in enumerate((total_ref.at[pl.ds(0, tokens), piece], gone_ref.at[:, piece])):
                    copy = pltpu.make_async_copy(source, outs[k].at[:, piece], out_sems.at[k, m])
                    leaving.append(copy)
                    copy.start()
    end(leaving)
    end(copies)


def expand(tokens, held, arena, slots, devices, loads, table, stored):
    width = arena.shape[1]
    shapes = []
    scratch = [pltpu.SemaphoreType.DMA((len(held),))]
    scratch += [pltpu.VMEM(operand.shape, operand.dtype) for operand in held]
    if devices:
        shapes = [jax.ShapeDtypeStruct((tokens, width), dtype) for dtype in (F32, BF16)]
        scratch.append(pltpu.SemaphoreType.DMA((2, len(spans(width)))))
        scratch += [pltpu.VMEM((2 * tokens, width), F32), pltpu.VMEM((tokens, width), BF16)]
    body = functools.partial(expand_body, slots, devices, tokens)
    *outs, arena = call(body, held, shapes, scratch, arena, loads, table, stored)
    return outs, arena


def swap(value, axis, bit):
    return lax.ppermute(value, axis, [(i, i ^ bit) for i in range(lax.axis_size(axis))])


def to_chip(value, k):
    count = lax.axis_size("ty")
    return lax.ppermute(value, "ty", [(i, (i + 2 * k) % count) for i in range(count)])


def cross_pipe(value, step, bit):
    sections, count = lax.axis_size("pipe"), lax.axis_size("tx")
    pairs = [
        (p * count + i, (p + step) % sections * count + (i ^ bit))
        for p in range(sections)
        for i in range(count)
    ]
    return lax.ppermute(value, ("pipe", "tx"), pairs)


def block_order(count):
    bits = count.bit_length() - 1
    return [int(format(n, f"0{bits}b")[::-1], 2) if bits else 0 for n in range(count)]


def finish(kept, got, t, ahead, back):
    count = lax.axis_size("tx")

    def across(value, bit):
        if lax.axis_size("pipe") == 2:
            return cross_pipe(value, 1, bit)
        return jnp.concatenate([cross_pipe(value[:t], 1, bit), cross_pipe(value[t:], -1, bit)])

    bit = 1
    while 2 * bit < count:
        kept = kept + got.astype(F32)
        half = kept.shape[0] // 2
        kept, gone = kept[:half], kept[half:].astype(BF16)
        bit *= 2
        if 2 * bit < count:
            got = swap(gone, "tx", bit)
    far = across(gone, bit)
    near = across(kept.astype(BF16), 0)
    total = near.astype(F32) + far.astype(F32)
    return (total[:t] + ahead.astype(F32)).astype(BF16), (total[t:] + back.astype(F32)).astype(BF16)


def gather_body(t, count, loads, *refs):
    operands, _, _, arena, _, copies = split(refs, loads, count, 0)
    begin(copies)
    shape = (3 * count * t, 3 * t)
    row = lax.broadcasted_iota(jnp.int32, shape, 0)
    column = lax.broadcasted_iota(jnp.int32, shape, 1)
    kind, row = row // (count * t), row % (count * t)
    source = kind * t + row % t
    picks = [
        jnp.where((row // t == i) & (column == source), 1.0, 0.0).astype(BF16) for i in range(count)
    ]
    base = arena.shape[0] - 7 * count * t
    for low, size in spans(arena.shape[1], 512):
        piece = pl.ds(low, size)
        rows = sum(contract(pick, operand[:, piece], NN) for pick, operand in zip(picks, operands))
        arena[pl.ds(base, shape[0]), piece] = rows.astype(BF16)
    end(copies)


def after(value, others):
    return lax.optimization_barrier((value, others))[0]


def gathered(section, saved, grads, shape, loads, table, stored):
    count = lax.axis_size("tx")
    t = section.shape[0]
    own = jnp.concatenate([section, saved, grads])
    bit = count // 2
    blocks, near = {0: own}, None
    if count > 1:
        near = swap(after(own, table), "tx", 1)
    arena = load(shape, loads[:-1], table, stored)
    later = after(own, arena)
    ahead = cross_pipe(later, 1, 0)
    back = ahead if lax.axis_size("pipe") == 2 else cross_pipe(later, -1, 0)
    while bit > 1:
        for i in list(blocks):
            blocks[i ^ bit] = swap(blocks[i], "tx", bit)
        bit //= 2
    if count > 1:
        far = [i for i in blocks if i]
        for i in far:
            blocks[i ^ 1] = swap(after(blocks[i], arena), "tx", 1)
        blocks[1] = near
    arena = load(arena, loads[-1:], table, stored)
    order = block_order(count)
    operands = [blocks[i] for i in order]
    body = functools.partial(gather_body, t, count)
    arena = call(body, operands, [], [], after(arena, (ahead, back)), [], table, stored, VM)[0]
    return arena, ahead[:t], back[2 * t :]


def residency(groups, quiet, slots, first):
    uses = [piece for group in groups for piece in group]

    def next_use(piece, at):
        return next((n for n in range(at, len(uses)) if uses[n] == piece), len(uses))

    begun = [(piece, slot, 0) for slot, piece in enumerate(list(dict.fromkeys(uses))[:first])]
    holds = {slot: None for slot in range(slots)}
    holds.update((slot, piece) for piece, slot, _ in begun)
    loads_at, slot_at, at = [], [], 0
    for step, group in enumerate(groups):
        slot_at.append([next(slot for slot, piece in holds.items() if piece == use) for use in group])
        loads = []
        later = at + len(group)
        for stage in range(len(group)):
            busy = slot_at[-1][stage:]
            while True:
                wanted = next((p for p in uses[later:] if p not in holds.values()), None)
                urgent = step + 1 < len(groups) and wanted in groups[step + 1]
                free = [s for s in holds if s not in busy and s not in [slot for _, slot, _ in loads]]
                if wanted is None or not free or (loads or step in quiet) and not urgent:
                    break
                slot = max(free, key=lambda s: next_use(holds[s], later))
                if next_use(holds[slot], later) <= next_use(wanted, later):
                    break
                loads.append((wanted, slot, stage))
                holds[slot] = wanted
        loads_at.append(loads)
        at += len(group)
    return begun, loads_at, slot_at


def local(section_input, saved_input, out_grad, gate_weight, up_weight, down_weight):
    count, tx = lax.axis_size("ty"), lax.axis_size("tx")
    chips = count // 2
    stored = [jnp.swapaxes(gate_weight[0], 0, 1), jnp.swapaxes(up_weight[0], 0, 1), down_weight[0]]
    units = up_to(stored[0].shape[0], 16)
    if units != stored[0].shape[0]:
        stored = [jnp.pad(w, ((0, units - w.shape[0]), (0, 0))) for w in stored]
    share = up_to(-(-units // count), 16)
    cut = share - share // 2 // 128 * 128
    subs = [(0, cut), (cut, share - cut)] if cut < share else [(0, share)]
    most = 3 * max(rows for _, rows in subs)

    me = lax.axis_index("ty")
    core, chip = me % 2, me // 2

    def share_of(k, mine):
        owner = (chip + k) % chips * 2 + (core if mine else 1 - core)
        return owner * share, jnp.minimum(owner * share, units - share)

    def place(k, mine, sub):
        return (share_of(k, mine)[1] + subs[sub][0]).astype(jnp.int32)

    def pieces(chip_order, core_order):
        return [(k, mine, sub) for k in chip_order for mine in core_order for sub in range(len(subs))]

    steps = [("project", [piece]) for piece in pieces(range(1, chips), (False, True)) + pieces((0,), (False,))]
    middle = len(steps) - len(subs) - 1
    if chips > 1:
        steps[middle : middle + 2] = [("project", steps[middle][1] + steps[middle + 1][1])]
    steps += [("activate", [piece]) for piece in pieces((0,), (True,))]
    near, far = pieces((0,), (False,)), pieces(range(1, chips), (True,))
    steps += [("expand", near[n : n + 1] + far[n : n + 1]) for n in range(max(len(near), len(far)))]
    left = pieces(range(1, chips), (False,))
    last = len(subs)
    steps += [("expand", left[n : min(n + 2, len(left) - last)]) for n in range(0, len(left) - last, 2)]
    steps.append(("end", left[-last:]))
    quiet = [n for n, (kind, group) in enumerate(steps) if kind == "project" and group[0][1] and len(group) == 1]
    begun, loads_at, slot_at = residency([group for _, group in steps], quiet, SLOTS, BEGUN)

    entries = {piece: n for n, piece in enumerate(pieces(range(chips), (False, True)))}
    share_at, within = share_of(0, True)
    table = jnp.stack(
        [place(*piece) for piece in entries]
        + [(share_at - within - at).astype(jnp.int32) for at, _ in subs]
    )

    def request(items):
        loads = [(slot * most, subs[piece[2]][1], entries[piece], stage) for piece, slot, stage in items]
        return loads, table, stored

    tokens = tx * section_input.shape[1]
    shape = (SLOTS * most + 7 * tokens, stored[0].shape[1])
    arena, ahead, back = gathered(section_input[0], saved_input[0], out_grad[0], shape, *request(begun))
    passed, arrived, h, forwarded = {}, {}, {}, chips == 1
    for n, (kind, group) in enumerate(steps):
        slots = [(slot * most, subs[piece[2]][1]) for slot, piece in zip(slot_at[n], group)]
        loads = request(loads_at[n])
        if kind in ("project", "activate"):
            jobs = []
            for slot, (k, mine, sub) in zip(slots, group):
                more = passed.pop((k, sub)) if mine else []
                if mine and not k:
                    jobs.append((slot, more, arrived.get(sub, []), (), F32, len(entries) + sub, not sub))
                else:
                    leave, dtype = ((5,), BF16) if mine else ((5,) if k or sub else SPLIT, F32)
                    jobs.append((slot, more, [], leave, dtype, None, False))
            parts, arena = project(tokens, arena, jobs, *loads)
            for k, mine, sub in group:
                if mine and not k:
                    own = parts.pop(0)
                    h[0, True, sub] = own
                    for i in range(1, chips):
                        h[i, True, sub] = to_chip(own, chips - i)
                    h[0, False, sub] = swap(own, "ty", 1)
                elif mine:
                    arrived.setdefault(sub, []).append(to_chip(parts.pop(0), k))
                else:
                    count = 1 if k or sub else len(SPLIT)
                    passed[k, sub] = [swap(parts.pop(0), "ty", 1) for _ in range(count)]
        elif kind == "expand":
            held = [h[piece] for piece in group]
            _, arena = expand(tokens, held, arena, slots, 0, *loads)
            if not forwarded and len(h) == len(subs) * (chips + 1):
                forwarded = True
                for i in range(1, chips):
                    for j in range(len(subs)):
                        h[i, False, j] = swap(after(h[i, True, j], arena), "ty", 1)
        else:
            if not forwarded:
                for i in range(1, chips):
                    for j in range(len(subs)):
                        h[i, False, j] = swap(h[i, True, j], "ty", 1)
            held = [h[piece] for piece in group]
            (kept, gone), _ = expand(tokens, held, arena, slots, tx, *loads)
            got = swap(gone, "tx", 1)
            next_input, prev_grad = finish(kept, got, section_input.shape[1], ahead, back)
    return (next_input[None], prev_grad[None])


def solution(mesh):
    return jax.shard_map(
        local,
        mesh=mesh,
        in_specs=(
            P("pipe", "tx", "ty"),
            P("pipe", "tx", "ty"),
            P("pipe", "tx", "ty"),
            P("pipe", "ty", "tx"),
            P("pipe", "ty", "tx"),
            P("pipe", "tx", "ty"),
        ),
        out_specs=(P("pipe", "tx", "ty"), P("pipe", "tx", "ty")),
        check_vma=False,
    )
```
